128 devices in a mesh: seq: 16 (over z, x), pair: 8 (over y, core).
Axes of the slice: x: 4, y: 4, z: 4, core: 2. Of those that a mesh axis runs over, the one named last changes fastest.
Arguments:
- queries: bfloat16 [32768, 1024], P(('seq', 'pair')), may hold values from -6 to 6
- keys: bfloat16 [32768, 1024], P(('seq', 'pair')), may hold values from -6 to 6
- values: bfloat16 [32768, 1024], P(('seq', 'pair')), may hold values from -6 to 6
- out_grad: bfloat16 [32768, 1024], P(('seq', 'pair')), may hold values from -6 to 6
- event_bucket: int32 [32768], P(('seq', 'pair')), may hold values from 0 to 63
- slope: float32 [8], replicated, may hold values from 0.02 to 0.5
- block_user: int32 [128], replicated, may hold values from 0 to 31, as said below
- lengths: int32 [32], replicated, may hold values from 1 to 2048, as said below
Outputs:
- attn_out: bfloat16 [32768, 1024], P(('seq', 'pair'))
- grad_query: bfloat16 [32768, 1024], P(('seq', 'pair'))
- grad_key: bfloat16 [32768, 1024], P(('seq', 'pair'))
- grad_value: bfloat16 [32768, 1024], P(('seq', 'pair'))
The draws below stay inside these ranges and needn't reach their ends.
Inputs may be any that keep to these rules, and one draw needn't show every extreme that they name: `block_user`: Nondecreasing; every user owns between 1 and 8 consecutive blocks, users in increasing order. A user owning c blocks has 256 * (c - 1) < lengths[u] <= 256 * c.
All inputs are finite; a program needn't handle non-finite values.
Results may differ from the reference program's by a relative error of at most 0.005.
Values may be sent and summed in bfloat16 or wider, within the bound.
A program may use at most 128 MiB of HBM per device.

```python
import math
import jax
import jax.numpy as jnp
from jax import lax

HEADS = 8
BLK = 256
MAXB = 8
D = 1024
NBLK = 128
EVENTS = 32768
USERS = 32


block_patterns = [[8, 4, 2, 2], [8, 6, 1, 1], [5, 4, 4, 3], [7, 5, 3, 1], [6, 6, 2, 2], [4, 4, 4, 4], [8, 5, 2, 1], [3, 3, 5, 5]]


def history_blocks(key):
    quartets = USERS // 4
    picks = jax.random.randint(key, (quartets,), 0, 8)
    picks = jnp.where(jnp.arange(quartets) == 0, 0, picks)
    pattern_table = jnp.array(block_patterns, dtype=jnp.int32)
    counts = pattern_table[picks].reshape(-1)
    shuffle = jax.random.permutation(jax.random.fold_in(key, 7), USERS)
    return counts[shuffle].astype(jnp.int32)


def draw_block_user(key, part):
    counts = history_blocks(key)
    block_ends = jnp.cumsum(counts)
    blocks = jnp.arange(NBLK, dtype=jnp.int32)
    return jnp.sum((block_ends[None, :] <= blocks[:, None]).astype(jnp.int32), axis=1).astype(jnp.int32)


def draw_lengths(key, part):
    counts = history_blocks(key)
    key = jax.random.fold_in(key, 13)
    final_fill = jax.random.randint(key, (USERS,), 1, BLK + 1)
    final_fill = jnp.where(counts == MAXB, BLK, final_fill)
    return ((counts - 1) * BLK + final_fill).astype(jnp.int32)


def set_ends(drawn, key, low, top_value):
    shape = drawn.shape
    index_at = [jax.random.randint(jax.random.fold_in(key, axis), (), 0, shape[axis]) for axis in range(len(shape))]
    drawn = drawn.at[tuple(index_at)].set(low)
    longest = shape.index(max(shape))
    index_at[longest] = (index_at[longest] + 1) % shape[longest]
    return drawn.at[tuple(index_at)].set(top_value)


def shard_levels(key, dims, split, low, largest):
    factor_of, own = 1.0, jax.random.fold_in(key, 6)
    for axis_at, blocks in split:
        steps = jnp.exp(jax.random.uniform(jax.random.fold_in(own, axis_at), (blocks,), jnp.float32, low / len(split), largest / len(split)))
        factor_of = factor_of * jnp.repeat(steps, dims[axis_at] // blocks).reshape([-1 if axis == axis_at else 1 for axis in range(len(dims))])
    return factor_of


def bell_draw(rng, extent, deviation, limit, split=(), kind=jnp.bfloat16):
    gain = shard_levels(rng, extent, split, -0.22, 0.18) if split else 1.0
    result = jax.random.normal(rng, extent, jnp.float32) * deviation * gain
    return jnp.minimum(jnp.maximum(result, -limit), limit).astype(kind)


def setup_inputs(seed: int = 0) -> dict:
    seeds = jax.random.split(jax.random.key(seed), 9)
    queries = bell_draw(seeds[0], (EVENTS, D), 1.0, 6.0, ((0, 128),))
    keys = bell_draw(seeds[1], (EVENTS, D), 1.0, 6.0, ((0, 128),))
    values = bell_draw(seeds[2], (EVENTS, D), 1.0, 6.0, ((0, 128),))
    out_grad = bell_draw(seeds[3], (EVENTS, D), 1.0, 6.0, ((0, 128),))
    event_bucket = set_ends(jax.random.randint(seeds[4], (EVENTS,), 0, 64), jax.random.fold_in(seeds[4], 1), 0, 63).astype(jnp.int32)
    slope = jnp.clip(jnp.exp(jax.random.uniform(seeds[5], (HEADS,), jnp.float32, math.log(0.02), math.log(0.5))), 0.02, 0.5)
    block_user = draw_block_user(jax.random.fold_in(seeds[8], 71), 0)
    lengths = draw_lengths(jax.random.fold_in(seeds[8], 71), 0)
    return {"queries": queries, "keys": keys, "values": values, "out_grad": out_grad, "event_bucket": event_bucket, "slope": slope, "block_user": block_user, "lengths": lengths}


def event_info(block_index, block_user, lengths, block_span):
    block_count = block_user.shape[0]
    user_count = lengths.shape[0]
    inside = (block_index >= 0) & (block_index < block_count)
    matches = block_index[:, None] == jnp.arange(block_count, dtype=jnp.int32)[None, :]
    block_owner = jnp.sum(jnp.where(matches, block_user[None, :], 0), axis=1).astype(jnp.int32)
    first_block = jnp.sum((block_user[None, :] < block_owner[:, None]).astype(jnp.int32), axis=1)
    picked = jnp.arange(user_count, dtype=jnp.int32)[None, :] == block_owner[:, None]
    history = jnp.sum(jnp.where(picked, lengths[None, :], 0), axis=1).astype(jnp.int32)
    offsets = jnp.arange(block_span, dtype=jnp.int32)
    position = (block_index - first_block)[:, None] * block_span + offsets[None, :]
    usable = inside[:, None] & (position < history[:, None])
    global_event = block_index[:, None] * block_span + offsets[None, :]
    owner_rows = block_owner[:, None] + 0 * offsets[None, :]
    length_rows = history[:, None] + 0 * offsets[None, :]
    return owner_rows.reshape(-1), usable.reshape(-1), global_event.reshape(-1), length_rows.reshape(-1)


def tile_grads(query_rows, key_rows, value_rows, grad_rows, weight, time_gap, slope):
    row_count, full_width = query_rows.shape
    key_count = key_rows.shape[0]
    head_count = slope.shape[0]
    head_dim = full_width // head_count
    score_scale = head_dim ** -0.5
    query_heads = query_rows.astype(jnp.float32).reshape(row_count, head_count, head_dim)
    key_heads = key_rows.astype(jnp.float32).reshape(key_count, head_count, head_dim)
    value_heads = value_rows.astype(jnp.float32).reshape(key_count, head_count, head_dim)
    grad_heads = grad_rows.astype(jnp.float32).reshape(row_count, head_count, head_dim)
    scores = jnp.einsum("qhd,khd->hqk", query_heads, key_heads) * score_scale - slope[:, None, None] * time_gap[None]
    squash = jax.nn.sigmoid(scores)
    attn = (scores * squash * weight[None]).astype(jnp.bfloat16)
    attn_wide = lax.optimization_barrier(attn).astype(jnp.float32)
    output = jnp.einsum("hqk,khd->qhd", attn_wide, value_heads)
    d_attn = jnp.einsum("qhd,khd->hqk", grad_heads, value_heads)
    d_score = (d_attn * weight[None] * (squash * (1.0 + scores * (1.0 - squash)))).astype(jnp.bfloat16)
    score_wide = lax.optimization_barrier(d_score).astype(jnp.float32)
    grad_q = jnp.einsum("hqk,khd->qhd", score_wide, key_heads) * score_scale
    grad_k = jnp.einsum("hqk,qhd->khd", score_wide, query_heads) * score_scale
    grad_v = jnp.einsum("hqk,qhd->khd", attn_wide, grad_heads)
    return (output.reshape(row_count, full_width), grad_q.reshape(row_count, full_width),
            grad_k.reshape(key_count, full_width), grad_v.reshape(key_count, full_width))


def reference(queries, keys, values, out_grad, event_bucket, slope, block_user, lengths):
    total_events, full_width = queries.shape
    block_count = total_events // BLK
    margin = (MAXB - 1) * BLK
    padded_keys = jnp.concatenate([jnp.zeros((margin, full_width), keys.dtype), keys], axis=0)
    padded_values = jnp.concatenate([jnp.zeros((margin, full_width), values.dtype), values], axis=0)
    padded_bucket = jnp.concatenate([jnp.zeros((margin,), jnp.int32), event_bucket], axis=0)

    def one_block(running, block_index):
        start = block_index * BLK
        query_rows = lax.dynamic_slice_in_dim(queries, start, BLK, 0)
        grad_rows = lax.dynamic_slice_in_dim(out_grad, start, BLK, 0)
        bucket_rows = lax.dynamic_slice_in_dim(event_bucket, start, BLK, 0)
        key_rows = lax.dynamic_slice_in_dim(padded_keys, start, MAXB * BLK, 0)
        value_rows = lax.dynamic_slice_in_dim(padded_values, start, MAXB * BLK, 0)
        key_bucket = lax.dynamic_slice_in_dim(padded_bucket, start, MAXB * BLK, 0)
        query_blocks = jnp.reshape(block_index, (1,)).astype(jnp.int32)
        key_blocks = (block_index - (MAXB - 1) + jnp.arange(MAXB, dtype=jnp.int32)).astype(jnp.int32)
        q_owner, q_usable, q_global, q_length = event_info(query_blocks, block_user, lengths, BLK)
        k_owner, k_usable, k_global, k_length = event_info(key_blocks, block_user, lengths, BLK)
        visible = q_usable[:, None] & k_usable[None, :] & (q_owner[:, None] == k_owner[None, :]) & (k_global[None, :] <= q_global[:, None])
        weight = jnp.where(visible, 1.0 / q_length.astype(jnp.float32)[:, None], jnp.float32(0.0)).astype(jnp.float32)
        time_gap = jnp.abs(bucket_rows.astype(jnp.float32)[:, None] - key_bucket.astype(jnp.float32)[None, :])
        output, grad_q, grad_k, grad_v = tile_grads(query_rows, key_rows, value_rows, grad_rows, weight, time_gap, slope)
        summed_key, summed_value = running
        summed_key = lax.dynamic_update_slice_in_dim(summed_key, lax.dynamic_slice_in_dim(summed_key, start, MAXB * BLK, 0) + grad_k, start, 0)
        summed_value = lax.dynamic_update_slice_in_dim(summed_value, lax.dynamic_slice_in_dim(summed_value, start, MAXB * BLK, 0) + grad_v, start, 0)
        return (summed_key, summed_value), (output.astype(jnp.bfloat16), grad_q.astype(jnp.bfloat16))

    running = (jnp.zeros((margin + total_events, full_width), jnp.float32), jnp.zeros((margin + total_events, full_width), jnp.float32))
    final, stacked = lax.scan(one_block, running, jnp.arange(block_count, dtype=jnp.int32))
    attn_out = stacked[0].reshape(total_events, full_width)
    grad_query = stacked[1].reshape(total_events, full_width)
    grad_key = final[0][margin:].astype(jnp.bfloat16)
    grad_value = final[1][margin:].astype(jnp.bfloat16)
    return (attn_out, grad_query, grad_key, grad_value)
```

```python
import functools

import jax
import jax.numpy as jnp
from jax import lax
from jax.experimental import pallas as pl
from jax.experimental.pallas import tpu as pltpu
from jax.sharding import PartitionSpec as P

BLK = 256
HD = 128
RING = 8
MESH = pl.DeviceIdType.MESH
f32, bf16, i32 = jnp.float32, jnp.bfloat16, jnp.int32
SCALE = HD ** -0.5
NN = (((1,), (0,)), ((), ()))
NT = (((1,), (1,)), ((), ()))


def dot(a, b, dims=NN):
    return lax.dot_general(a, b, dims, preferred_element_type=f32)


def kernel(
    seqs, slope_ref, user_ref, length_ref, bucket_ref, q_hbm, k_hbm, v_hbm, g_hbm,
    o_out, dq_out, dk_out, dv_out,
    QB, KB, VB, GB, G_own, B_own, B_ring, B_cross, colB, rowB, inv,
    OJ, QJ, VI, KI, FJU, FJW, FIU, FIW,
    stage, cross_out, cross_in,
    load_sem, self_sem, in_send, in_recv, b_send, b_recv, x_send, x_recv, r_send, r_recv, o_send, o_recv, o_self,
):
    seq, pair = lax.axis_index("seq"), lax.axis_index("pair")
    blocks = seqs * RING
    y, core = pair // 2, pair % 2
    up, down = (seq + 1) % seqs, (seq + seqs - 1) % seqs
    outs = (o_out, dq_out, dk_out, dv_out)
    rings = (QB, KB, VB, GB)

    def place(k):
        return ((y + k // 2) % 4) * 2 + (core + k % 2) % 2

    def source(k):
        return ((y + 4 - k // 2) % 4) * 2 + (core + k % 2) % 2

    barrier = pltpu.get_barrier_semaphore()

    def greet(k, _):
        pl.semaphore_signal(barrier, inc=1, device_id=(seq, place(k)), device_id_type=MESH)
        return 0

    lax.fori_loop(1, RING, greet, 0)
    pl.semaphore_signal(barrier, inc=1, device_id=(up, pair), device_id_type=MESH)
    pl.semaphore_signal(barrier, inc=1, device_id=(down, pair), device_id_type=MESH)

    load = pltpu.make_async_copy(g_hbm, G_own, load_sem)
    load.start()

    def block_user(block):
        return user_ref[jnp.clip(block, 0, blocks - 1)]

    def live_rows(block):
        user = block_user(block)
        last = (block == blocks - 1) | (block_user(block + 1) != user)
        return jnp.where(last, lax.rem(length_ref[user] - 1, BLK) + 1, BLK)

    def prepare(p, _):
        zero = jnp.zeros((BLK, HD), f32)
        OJ[p] = zero
        QJ[p] = zero
        FJU[p] = zero
        FJW[p] = zero
        zero = jnp.zeros((HD, BLK), f32)
        VI[p] = zero
        KI[p] = zero
        FIU[p] = zero
        FIW[p] = zero

        @pl.when(p < 3)
        def _():
            FIU[8 + p] = zero
            FIW[8 + p] = zero

        length = length_ref[block_user(RING * seq + p)]
        inv[p] = 1.0 / jnp.full((8, BLK), length.astype(f32), f32)
        return 0

    lax.fori_loop(0, RING, prepare, 0)
    B_own[...] = jnp.broadcast_to(bucket_ref[...].astype(f32).reshape(1, BLK), (8, BLK))
    load.wait()
    own_live = live_rows(RING * seq + pair)

    def mask_own(n, _):
        rows = pl.ds(pl.multiple_of(n * 32, 32), 32)
        row = lax.broadcasted_iota(i32, (32, RING * HD), 0) + n * 32
        G_own[rows, :] = jnp.where(row < own_live, G_own[rows, :].astype(f32), 0.0).astype(bf16)
        return 0

    lax.fori_loop(0, BLK // 32, mask_own, 0)
    pl.semaphore_wait(barrier, RING + 1)

    sources = (q_hbm, k_hbm, v_hbm, G_own)

    def head(p):
        return pl.ds(pl.multiple_of(p * HD, HD), HD)

    def bucket_copy(k):
        return pltpu.make_async_remote_copy(
            B_own, B_ring.at[pair], b_send.at[k], b_recv.at[pair], device_id=(seq, place(k)), device_id_type=MESH)

    def in_copy(t, k):
        p = place(k)
        return pltpu.make_async_remote_copy(
            sources[t].at[:, head(p)], rings[t].at[pair], in_send.at[t, k], in_recv.at[t, pair],
            device_id=(seq, p), device_id_type=MESH)

    def self_copy(t):
        return pltpu.make_async_copy(sources[t].at[:, head(pair)], rings[t].at[pair], self_sem.at[t])

    for t in range(4):
        self_copy(t).start()
    self_bucket = pltpu.make_async_copy(B_own, B_ring.at[pair], self_sem.at[4])
    self_bucket.start()

    def send_two(first, second):
        def body(k, _):
            in_copy(first, k).start()
            in_copy(second, k).start()
            return 0

        lax.fori_loop(1, RING, body, 0)

    def send_buckets(k, _):
        bucket_copy(k).start()
        return 0

    lax.fori_loop(1, RING, send_buckets, 0)

    @pl.when(pair >= 4)
    def _():
        send_two(1, 2)
        send_two(0, 3)

    @pl.when(pair < 4)
    def _():
        send_two(0, 3)
        send_two(1, 2)

    for t in range(4):
        self_copy(t).wait()
    self_bucket.wait()

    def wait_in(t, p):
        pltpu.make_async_copy(rings[t].at[p], rings[t].at[p], in_recv.at[t, p]).wait()

    def cross_copies(p, upward):
        if upward:
            pairs = ((KB.at[p], KB.at[p + 4]), (VB.at[p], VB.at[p + 4]), (B_ring.at[p], B_cross.at[p]))
            to = (up, pair)
        else:
            pairs = ((QB.at[p], QB.at[p + 8]), (GB.at[p], GB.at[p + 8]), (B_ring.at[p], B_cross.at[p]))
            to = (down, pair)
        return [
            pltpu.make_async_remote_copy(
                src, dst, x_send.at[n, p], x_recv.at[n, p], device_id=to, device_id_type=MESH)
            for n, (src, dst) in enumerate(pairs)
        ]

    def pass_on(k, _):
        p = source(k)

        @pl.when(k > 0)
        def _():
            pltpu.make_async_copy(B_ring.at[p], B_ring.at[p], b_recv.at[p]).wait()

        @pl.when(p >= 4)
        def _():
            @pl.when(k > 0)
            def _():
                wait_in(1, p)
                wait_in(2, p)

            for copy in cross_copies(p, True):
                copy.start()

        @pl.when(p < 4)
        def _():
            @pl.when(k > 0)
            def _():
                wait_in(0, p)
                wait_in(3, p)

            @pl.when(p < 3)
            def _():
                for copy in cross_copies(p, False):
                    copy.start()

        return 0

    lax.fori_loop(0, RING, pass_on, 0)

    half_slope = 0.5 * slope_ref[pair]

    def arrive(k):
        p = source(k)

        @pl.when(k > 0)
        def _():
            @pl.when(p >= 4)
            def _():
                wait_in(0, p)
                wait_in(3, p)

            @pl.when(p < 4)
            def _():
                wait_in(1, p)
                wait_in(2, p)

        row = B_ring[p] * half_slope
        rowB[p] = row
        colB[p] = jnp.broadcast_to(row[0:1], (HD, BLK)).T

        @pl.when(p >= 4)
        def _():
            for copy in cross_copies(p, True):
                copy.wait_recv()
            crossed = B_cross[p] * half_slope
            colB[p + 4] = jnp.broadcast_to(crossed[0:1], (HD, BLK)).T

        @pl.when(p < 3)
        def _():
            for copy in cross_copies(p, False):
                copy.wait_recv()
            rowB[p + 8] = B_cross[p] * half_slope

    def tile(xj, yj, xi, yi, column, row, weight, mask=None):
        gap = jnp.abs(jnp.concatenate([column, column], axis=1) - row)
        half = dot(xj, xi, NT) * (0.5 * SCALE) - gap
        th = jnp.tanh(half)
        pw = th * weight + weight
        if mask is not None:
            pw = jnp.where(mask, pw, 0.0)
        aw = half * pw
        attn = aw.astype(bf16)
        bend = pw + aw * (1.0 - th)
        score = (dot(yj, yi, NT) * bend).astype(bf16)
        return (dot(attn, yi), dot(score, xi), dot(yj.T, attn), dot(xj.T, score))

    def diagonal(p):
        mask = lax.broadcasted_iota(i32, (BLK, BLK), 0) >= lax.broadcasted_iota(i32, (BLK, BLK), 1)
        uj, wj, ui, wi = tile(QB[p], GB[p], KB[p], VB[p], colB[p], rowB[p][0:1], inv[p][0:1], mask)
        OJ[p] += uj
        QJ[p] += wj
        VI[p] += ui
        KI[p] += wi

    def slot(p, r):
        j, i = jnp.maximum(p, r), jnp.minimum(p, r)
        upper = j >= 4
        ja = jnp.where(upper, j + 4, j)
        ia = jnp.where(upper, i, i + 8)
        base = RING * seq
        user_i, user_j = block_user(base + i), block_user(base + j)
        inside = user_i == user_j
        below = (block_user(base + j - 8) == user_i) & (seq > 0)
        above = (block_user(base + i + 8) == user_j) & (seq < seqs - 1)
        flag = jnp.where(upper, below, above)
        valid = jnp.where(inside | flag, 1.0, 0.0)
        on = jnp.where(flag, 1.0, 0.0)
        off = 1.0 - on
        weight = inv[jnp.where(upper, i, j)][0:1] * valid

        def pick(a, b):
            return lax.select(flag, a, b)

        uj, wj, ui, wi = tile(
            pick(KB[ja], QB[j]), pick(VB[ja], GB[j]), pick(QB[ia], KB[i]), pick(GB[ia], VB[i]),
            pick(colB[ja], colB[j]), pick(rowB[ia], rowB[i])[0:1], weight)
        OJ[j] += uj * off
        QJ[j] += wj * off
        FJU[j] += uj * on
        FJW[j] += wj * on
        VI[i] += ui * off
        KI[i] += wi * off
        FIU[ia] += ui * on
        FIW[ia] += wi * on

    back = 0.5 * SCALE

    def out_copy(t, p):
        return pltpu.make_async_remote_copy(
            stage.at[t, p], outs[t].at[:, head(pair)], o_send.at[t, p], o_recv.at[t, pair],
            device_id=(seq, p), device_id_type=MESH)

    def out_self(t):
        return pltpu.make_async_copy(stage.at[t, pair], outs[t].at[:, head(pair)], o_self.at[t])

    def emit(t, p):
        @pl.when(p != pair)
        def _():
            out_copy(t, p).start()

        @pl.when(p == pair)
        def _():
            out_self(t).start()

    def return_copies(p, downward):
        to = (down, pair) if downward else (up, pair)
        return [
            pltpu.make_async_remote_copy(
                cross_out.at[n, p], cross_in.at[n, p], r_send.at[n, p], r_recv.at[n, p],
                device_id=to, device_id_type=MESH)
            for n in range(2)
        ]

    def live_mask(p):
        return lax.broadcasted_iota(i32, (BLK, HD), 0) < live_rows(RING * seq + p)

    def finish(p):
        o = OJ[p] + FIU[p].T
        dq = (QJ[p] + FIW[p].T) * back
        dv = VI[p].T
        dk = KI[p].T * back

        @pl.when(p >= 4)
        def _():
            cross_out[0, p] = FJU[p].astype(bf16)
            cross_out[1, p] = (FJW[p] * back).astype(bf16)
            for copy in return_copies(p, True):
                copy.start()
            FJU[p] = dv
            FJW[p] = dk

        @pl.when(p < 3)
        def _():
            cross_out[0, p] = FIU[p + 8].T.astype(bf16)
            cross_out[1, p] = (FIW[p + 8].T * back).astype(bf16)
            for copy in return_copies(p, False):
                copy.start()
            OJ[p] = o
            QJ[p] = dq

        @pl.when(p >= 3)
        def _():
            stage[0, p] = jnp.where(live_mask(p), o, 0.0).astype(bf16)
            stage[1, p] = dq.astype(bf16)
            emit(0, p)
            emit(1, p)

        @pl.when(p < 4)
        def _():
            stage[2, p] = (dk + FJW[p] * back).astype(bf16)
            stage[3, p] = (dv + FJU[p]).astype(bf16)
            emit(2, p)
            emit(3, p)

    def step(k, _):
        arrive(k)
        p = source(k)

        def two(m, _):
            slot(p, source(2 * m))
            slot(p, source(2 * m + 1))
            return 0

        lax.fori_loop(0, k // 2, two, 0)

        @pl.when(k % 2 == 1)
        def _():
            slot(p, source(k - 1))
            diagonal(p)

        @pl.when(k % 2 == 0)
        def _():
            diagonal(p)

        return 0

    lax.fori_loop(0, RING - 1, step, 0)
    arrive(RING - 1)
    last = source(RING - 1)

    def last_two(m, _):
        slot(last, source(2 * m))
        slot(last, source(2 * m + 1))
        finish(source(2 * m))
        finish(source(2 * m + 1))
        return 0

    lax.fori_loop(0, 3, last_two, 0)
    slot(last, source(6))
    diagonal(last)
    finish(source(6))
    finish(last)

    def settle(k, _):
        p = source(k)

        @pl.when(p >= 4)
        def _():
            for copy in return_copies(p, True):
                copy.wait_recv()
            stage[2, p] = (FJW[p] + cross_in[1, p].astype(f32)).astype(bf16)
            stage[3, p] = (FJU[p] + cross_in[0, p].astype(f32)).astype(bf16)
            emit(2, p)
            emit(3, p)

        @pl.when(p < 3)
        def _():
            for copy in return_copies(p, False):
                copy.wait_recv()
            stage[0, p] = jnp.where(live_mask(p), OJ[p] + cross_in[0, p].astype(f32), 0.0).astype(bf16)
            stage[1, p] = (QJ[p] + cross_in[1, p].astype(f32)).astype(bf16)
            emit(0, p)
            emit(1, p)

        return 0

    lax.fori_loop(0, RING, settle, 0)

    def drain(k, _):
        p = source(k)

        @pl.when(p >= 4)
        def _():
            for copy in cross_copies(p, True) + return_copies(p, True):
                copy.wait_send()

        @pl.when(p < 3)
        def _():
            for copy in cross_copies(p, False) + return_copies(p, False):
                copy.wait_send()

        @pl.when(k > 0)
        def _():
            bucket_copy(k).wait_send()
            for t in range(4):
                in_copy(t, k).wait_send()
                out_copy(t, p).wait_send()
                pltpu.make_async_copy(stage.at[t, p], outs[t].at[:, head(p)], o_recv.at[t, p]).wait()

        return 0

    lax.fori_loop(0, RING, drain, 0)
    for t in range(4):
        out_self(t).wait()


def per_device(seqs, queries, keys, values, out_grad, event_bucket, slope, block_user, lengths):
    wide = jax.ShapeDtypeStruct((BLK, RING * HD), bf16)
    smem = pl.BlockSpec(memory_space=pltpu.SMEM)
    vmem = pl.BlockSpec(memory_space=pltpu.VMEM)
    hbm = pl.BlockSpec(memory_space=pl.ANY)
    down = lambda n: pltpu.VMEM((n, BLK, HD), f32)
    across = lambda n: pltpu.VMEM((n, HD, BLK), f32)
    dma = pltpu.SemaphoreType.DMA
    return pl.pallas_call(
        functools.partial(kernel, seqs),
        out_shape=(wide,) * 4,
        in_specs=[smem, smem, smem, vmem, hbm, hbm, hbm, hbm],
        out_specs=(hbm,) * 4,
        scratch_shapes=[
            pltpu.VMEM((11, BLK, HD), bf16),
            pltpu.VMEM((12, BLK, HD), bf16),
            pltpu.VMEM((12, BLK, HD), bf16),
            pltpu.VMEM((11, BLK, HD), bf16),
            pltpu.VMEM((BLK, RING * HD), bf16),
            pltpu.VMEM((8, BLK), f32),
            pltpu.VMEM((8, 8, BLK), f32),
            pltpu.VMEM((8, 8, BLK), f32),
            down(12),
            pltpu.VMEM((11, 8, BLK), f32),
            pltpu.VMEM((8, 8, BLK), f32),
            down(8), down(8), across(8), across(8), down(8), down(8), across(11), across(11),
            pltpu.VMEM((4, 8, BLK, HD), bf16),
            pltpu.VMEM((2, 8, BLK, HD), bf16),
            pltpu.VMEM((2, 8, BLK, HD), bf16),
            dma, dma((5,)), dma((4, 8)), dma((4, 8)), dma((8,)), dma((8,)), dma((3, 8)), dma((3, 8)),
            dma((2, 8)), dma((2, 8)), dma((4, 8)), dma((4, 8)), dma((4,)),
        ],
        compiler_params=pltpu.CompilerParams(
            collective_id=0, has_side_effects=True, vmem_limit_bytes=48 * 2**20),
        cost_estimate=pl.CostEstimate(
            flops=36 * 6 * 2 * BLK * BLK * HD, bytes_accessed=8 * BLK * RING * HD * 2, transcendentals=36 * BLK * BLK),
    )(slope, block_user, lengths, event_bucket, queries, keys, values, out_grad)


def solution(mesh):
    spread = P(("seq", "pair"), None)
    return jax.shard_map(
        functools.partial(per_device, mesh.shape["seq"]),
        mesh=mesh,
        in_specs=(spread, spread, spread, spread, P(("seq", "pair")), P(), P(), P()),
        out_specs=(spread,) * 4,
        check_vma=False,
    )
```

```python
import functools

import jax
import jax.numpy as jnp
from jax import lax
from jax.experimental import pallas as pl
from jax.experimental.pallas import tpu as pltpu
from jax.sharding import PartitionSpec as P

BLK = 256
HD = 128
RING = 8
WHOLE = 5
MESH = pl.DeviceIdType.MESH
f32, bf16, i32 = jnp.float32, jnp.bfloat16, jnp.int32
SCALE = HD ** -0.5
NN = (((1,), (0,)), ((), ()))
NT = (((1,), (1,)), ((), ()))


def dot(a, b, dims=NN):
    return lax.dot_general(a, b, dims, preferred_element_type=f32)


def kernel(
    seqs, slope_hbm, user_hbm, length_hbm, bucket_hbm, q_hbm, k_hbm, v_hbm, g_hbm,
    o_out, dq_out, dk_out, dv_out,
    slope_ref, user_ref, length_ref, bucket_ref, QB, KB, VB, GB, G_own, B_own, B_ring, B_cross, colB, rowB, inv,
    OJ, QJ, VI, KI, FJU, FJW, FIU, FIW,
    stage, cross_out, cross_in,
    load_sem, small_sem, self_sem, in_send, in_recv, b_send, b_recv, x_send, x_recv, r_send, r_recv, o_send, o_recv, o_self,
):
    seq, pair = lax.axis_index("seq"), lax.axis_index("pair")
    blocks = seqs * RING
    y, core = pair // 2, pair % 2
    up, down = (seq + 1) % seqs, (seq + seqs - 1) % seqs
    outs = (o_out, dq_out, dk_out, dv_out)
    rings = (QB, KB, VB, GB)

    def offset(k):
        dy = jnp.where(k < 2, 0, jnp.where(k < 6, 1 + 2 * (k % 2), 2))
        dc = jnp.where(k < 2, k, jnp.where(k < 6, k // 4, k - 6))
        return dy, dc

    def place(k):
        dy, dc = offset(k)
        return ((y + dy) % 4) * 2 + (core + dc) % 2

    def source(k):
        dy, dc = offset(k)
        return ((y + 4 - dy) % 4) * 2 + (core + dc) % 2

    barrier = pltpu.get_barrier_semaphore()

    def greet(k, _):
        pl.semaphore_signal(barrier, inc=1, device_id=(seq, place(k)), device_id_type=MESH)
        return 0

    lax.fori_loop(1, RING, greet, 0)
    pl.semaphore_signal(barrier, inc=1, device_id=(up, pair), device_id_type=MESH)
    pl.semaphore_signal(barrier, inc=1, device_id=(down, pair), device_id_type=MESH)

    load = pltpu.make_async_copy(g_hbm, G_own, load_sem)
    load.start()
    smalls = [
        pltpu.make_async_copy(src, dst, small_sem.at[n])
        for n, (src, dst) in enumerate((
            (user_hbm, user_ref), (length_hbm, length_ref), (slope_hbm, slope_ref), (bucket_hbm, bucket_ref)))
    ]
    for small in smalls:
        small.start()
    for small in smalls:
        small.wait()

    def block_user(block):
        return user_ref[jnp.clip(block, 0, blocks - 1)]

    def live_rows(block):
        user = block_user(block)
        last = (block == blocks - 1) | (block_user(block + 1) != user)
        return jnp.where(last, lax.rem(length_ref[user] - 1, BLK) + 1, BLK)

    def prepare(p, _):
        zero = jnp.zeros((BLK, HD), f32)
        OJ[p] = zero
        QJ[p] = zero
        FJU[p] = zero
        FJW[p] = zero
        zero = jnp.zeros((HD, BLK), f32)
        VI[p] = zero
        KI[p] = zero
        FIU[p] = zero
        FIW[p] = zero

        @pl.when(p < 3)
        def _():
            FIU[8 + p] = zero
            FIW[8 + p] = zero

        length = length_ref[block_user(RING * seq + p)]
        inv[p] = 1.0 / jnp.full((8, BLK), length.astype(f32), f32)
        return 0

    lax.fori_loop(0, RING, prepare, 0)
    B_own[...] = jnp.broadcast_to(bucket_ref[...].astype(f32).reshape(1, BLK), (8, BLK))
    load.wait()
    own_live = live_rows(RING * seq + pair)

    def mask_own(n, _):
        rows = pl.ds(pl.multiple_of(n * 32, 32), 32)
        row = lax.broadcasted_iota(i32, (32, RING * HD), 0) + n * 32
        G_own[rows, :] = jnp.where(row < own_live, G_own[rows, :].astype(f32), 0.0).astype(bf16)
        return 0

    lax.fori_loop(0, BLK // 32, mask_own, 0)
    pl.semaphore_wait(barrier, RING + 1)

    sources = (q_hbm, k_hbm, v_hbm, G_own)

    def head(p):
        return pl.ds(pl.multiple_of(p * HD, HD), HD)

    def bucket_copy(k):
        return pltpu.make_async_remote_copy(
            B_own, B_ring.at[pair], b_send.at[k], b_recv.at[pair], device_id=(seq, place(k)), device_id_type=MESH)

    def in_copy(t, k):
        p = place(k)
        return pltpu.make_async_remote_copy(
            sources[t].at[:, head(p)], rings[t].at[pair], in_send.at[t, k], in_recv.at[t, pair],
            device_id=(seq, p), device_id_type=MESH)

    def self_copy(t):
        return pltpu.make_async_copy(sources[t].at[:, head(pair)], rings[t].at[pair], self_sem.at[t])

    for t in range(4):
        self_copy(t).start()
    self_bucket = pltpu.make_async_copy(B_own, B_ring.at[pair], self_sem.at[4])
    self_bucket.start()

    def send_order(first, second):
        def send(*tensors):
            def body(k, _):
                for t in tensors:
                    in_copy(t, k).start()
                return 0

            return body

        lax.fori_loop(1, WHOLE + 1, send(*first, *second), 0)
        lax.fori_loop(WHOLE + 1, RING, send(*first), 0)
        lax.fori_loop(WHOLE + 1, RING, send(*second), 0)

    def send_buckets(k, _):
        bucket_copy(k).start()
        return 0

    lax.fori_loop(1, RING, send_buckets, 0)

    @pl.when(pair >= 4)
    def _():
        send_order((1, 2), (0, 3))

    @pl.when(pair < 4)
    def _():
        send_order((0, 3), (1, 2))

    for t in range(4):
        self_copy(t).wait()
    self_bucket.wait()

    def wait_in(t, p):
        pltpu.make_async_copy(rings[t].at[p], rings[t].at[p], in_recv.at[t, p]).wait()

    def cross_copies(p, upward):
        if upward:
            pairs = ((KB.at[p], KB.at[p + 4]), (VB.at[p], VB.at[p + 4]), (B_ring.at[p], B_cross.at[p]))
            to = (up, pair)
        else:
            pairs = ((QB.at[p], QB.at[p + 8]), (GB.at[p], GB.at[p + 8]), (B_ring.at[p], B_cross.at[p]))
            to = (down, pair)
        return [
            pltpu.make_async_remote_copy(
                src, dst, x_send.at[n, p], x_recv.at[n, p], device_id=to, device_id_type=MESH)
            for n, (src, dst) in enumerate(pairs)
        ]

    def pass_on(k, _):
        p = source(k)

        @pl.when(k > 0)
        def _():
            pltpu.make_async_copy(B_ring.at[p], B_ring.at[p], b_recv.at[p]).wait()

        @pl.when(p >= 4)
        def _():
            @pl.when(k > 0)
            def _():
                wait_in(1, p)
                wait_in(2, p)

            for copy in cross_copies(p, True):
                copy.start()

        @pl.when(p < 4)
        def _():
            @pl.when(k > 0)
            def _():
                wait_in(0, p)
                wait_in(3, p)

            @pl.when(p < 3)
            def _():
                for copy in cross_copies(p, False):
                    copy.start()

        return 0


    half_slope = 0.5 * slope_ref[pair]

    def arrive(k):
        p = source(k)

        @pl.when(k > 0)
        def _():
            @pl.when(p >= 4)
            def _():
                wait_in(0, p)
                wait_in(3, p)

            @pl.when(p < 4)
            def _():
                wait_in(1, p)
                wait_in(2, p)

        row = B_ring[p] * half_slope
        rowB[p] = row
        colB[p] = jnp.broadcast_to(row[0:1], (HD, BLK)).T

        @pl.when(p >= 4)
        def _():
            for copy in cross_copies(p, True):
                copy.wait_recv()
            crossed = B_cross[p] * half_slope
            colB[p + 4] = jnp.broadcast_to(crossed[0:1], (HD, BLK)).T

        @pl.when(p < 3)
        def _():
            for copy in cross_copies(p, False):
                copy.wait_recv()
            rowB[p + 8] = B_cross[p] * half_slope

    def tile(xj, yj, xi, yi, column, row, weight, mask=None):
        gap = jnp.abs(jnp.concatenate([column, column], axis=1) - row)
        half = dot(xj, xi, NT) * (0.5 * SCALE) - gap
        th = jnp.tanh(half)
        pw = th * weight + weight
        if mask is not None:
            pw = jnp.where(mask, pw, 0.0)
        aw = half * pw
        attn = aw.astype(bf16)
        bend = pw + aw * (1.0 - th)
        score = (dot(yj, yi, NT) * bend).astype(bf16)
        return (dot(attn, yi), dot(score, xi), dot(yj.T, attn), dot(xj.T, score))

    def diagonal(p):
        mask = lax.broadcasted_iota(i32, (BLK, BLK), 0) >= lax.broadcasted_iota(i32, (BLK, BLK), 1)
        uj, wj, ui, wi = tile(QB[p], GB[p], KB[p], VB[p], colB[p], rowB[p][0:1], inv[p][0:1], mask)
        OJ[p] += uj
        QJ[p] += wj
        VI[p] += ui
        KI[p] += wi

    def slot(p, r):
        j, i = jnp.maximum(p, r), jnp.minimum(p, r)
        upper = j >= 4
        ja = jnp.where(upper, j + 4, j)
        ia = jnp.where(upper, i, i + 8)
        base = RING * seq
        user_i, user_j = block_user(base + i), block_user(base + j)
        inside = user_i == user_j
        below = (block_user(base + j - 8) == user_i) & (seq > 0)
        above = (block_user(base + i + 8) == user_j) & (seq < seqs - 1)
        flag = jnp.where(upper, below, above)
        valid = jnp.where(inside | flag, 1.0, 0.0)
        on = jnp.where(flag, 1.0, 0.0)
        off = 1.0 - on
        weight = inv[jnp.where(upper, i, j)][0:1] * valid

        def pick(a, b):
            return lax.select(flag, a, b)

        uj, wj, ui, wi = tile(
            pick(KB[ja], QB[j]), pick(VB[ja], GB[j]), pick(QB[ia], KB[i]), pick(GB[ia], VB[i]),
            pick(colB[ja], colB[j]), pick(rowB[ia], rowB[i])[0:1], weight)
        OJ[j] += uj * off
        QJ[j] += wj * off
        FJU[j] += uj * on
        FJW[j] += wj * on
        VI[i] += ui * off
        KI[i] += wi * off
        FIU[ia] += ui * on
        FIW[ia] += wi * on

    back = 0.5 * SCALE

    def out_copy(t, p):
        return pltpu.make_async_remote_copy(
            stage.at[t, p], outs[t].at[:, head(pair)], o_send.at[t, p], o_recv.at[t, pair],
            device_id=(seq, p), device_id_type=MESH)

    def out_self(t):
        return pltpu.make_async_copy(stage.at[t, pair], outs[t].at[:, head(pair)], o_self.at[t])

    def emit(t, p):
        @pl.when(p != pair)
        def _():
            out_copy(t, p).start()

        @pl.when(p == pair)
        def _():
            out_self(t).start()

    def return_copies(p, downward):
        to = (down, pair) if downward else (up, pair)
        return [
            pltpu.make_async_remote_copy(
                cross_out.at[n, p], cross_in.at[n, p], r_send.at[n, p], r_recv.at[n, p],
                device_id=to, device_id_type=MESH)
            for n in range(2)
        ]

    def live_mask(p):
        return lax.broadcasted_iota(i32, (BLK, HD), 0) < live_rows(RING * seq + p)

    def finish(p):
        o = OJ[p] + FIU[p].T
        dq = (QJ[p] + FIW[p].T) * back
        dv = VI[p].T
        dk = KI[p].T * back

        @pl.when(p >= 4)
        def _():
            cross_out[0, p] = FJU[p].astype(bf16)
            cross_out[1, p] = (FJW[p] * back).astype(bf16)
            for copy in return_copies(p, True):
                copy.start()
            FJU[p] = dv
            FJW[p] = dk

        @pl.when(p < 3)
        def _():
            cross_out[0, p] = FIU[p + 8].T.astype(bf16)
            cross_out[1, p] = (FIW[p + 8].T * back).astype(bf16)
            for copy in return_copies(p, False):
                copy.start()
            OJ[p] = o
            QJ[p] = dq

        @pl.when(p >= 3)
        def _():
            stage[0, p] = jnp.where(live_mask(p), o, 0.0).astype(bf16)
            stage[1, p] = dq.astype(bf16)
            emit(0, p)
            emit(1, p)

        @pl.when(p < 4)
        def _():
            stage[2, p] = (dk + FJW[p] * back).astype(bf16)
            stage[3, p] = (dv + FJU[p]).astype(bf16)
            emit(2, p)
            emit(3, p)

    def step(k, _):
        arrive(k)
        p = source(k)

        def two(m, _):
            slot(p, source(2 * m))
            slot(p, source(2 * m + 1))
            return 0

        lax.fori_loop(0, k // 2, two, 0)

        @pl.when(k % 2 == 1)
        def _():
            slot(p, source(k - 1))
            diagonal(p)

        @pl.when(k % 2 == 0)
        def _():
            diagonal(p)

        return 0

    def advance(k, _):
        first = jnp.where(k == 0, 0, jnp.where(k < 4, 4, jnp.where(k < 6, k, 7)))
        first = jnp.where(k == 5, 6, first)
        end = jnp.where(k < 4, 4, jnp.where(k == 4, 6, jnp.where(k == 5, 7, 8)))
        lax.fori_loop(first, end, pass_on, 0)
        step(k, 0)
        return 0

    lax.fori_loop(0, RING - 1, advance, 0)
    arrive(RING - 1)
    last = source(RING - 1)

    def turn(m):
        return source(jnp.where(m < 5, m + 2, 6 - m))

    def last_two(m, _):
        one, two = turn(2 * m), turn(2 * m + 1)
        slot(last, one)
        slot(last, two)
        finish(one)
        finish(two)
        return 0

    lax.fori_loop(0, 3, last_two, 0)
    slot(last, turn(6))
    diagonal(last)
    finish(last)
    finish(turn(6))

    def drain_in(k, _):
        p = source(k)

        @pl.when(p >= 4)
        def _():
            for copy in cross_copies(p, True):
                copy.wait_send()

        @pl.when(p < 3)
        def _():
            for copy in cross_copies(p, False):
                copy.wait_send()

        @pl.when(k > 0)
        def _():
            bucket_copy(k).wait_send()
            for t in range(4):
                in_copy(t, k).wait_send()

        return 0

    lax.fori_loop(0, RING, drain_in, 0)

    def settle(k, _):
        p = source((k + 2) % RING)

        @pl.when(p >= 4)
        def _():
            for copy in return_copies(p, True):
                copy.wait_recv()
            stage[2, p] = (FJW[p] + cross_in[1, p].astype(f32)).astype(bf16)
            stage[3, p] = (FJU[p] + cross_in[0, p].astype(f32)).astype(bf16)
            emit(2, p)
            emit(3, p)

        @pl.when(p < 3)
        def _():
            for copy in return_copies(p, False):
                copy.wait_recv()
            stage[0, p] = jnp.where(live_mask(p), OJ[p] + cross_in[0, p].astype(f32), 0.0).astype(bf16)
            stage[1, p] = (QJ[p] + cross_in[1, p].astype(f32)).astype(bf16)
            emit(0, p)
            emit(1, p)

        return 0

    lax.fori_loop(0, RING, settle, 0)

    def drain_out(k, _):
        p = source(k)

        @pl.when(p >= 4)
        def _():
            for copy in return_copies(p, True):
                copy.wait_send()

        @pl.when(p < 3)
        def _():
            for copy in return_copies(p, False):
                copy.wait_send()

        @pl.when(k > 0)
        def _():
            for t in range(4):
                out_copy(t, p).wait_send()
                pltpu.make_async_copy(stage.at[t, p], outs[t].at[:, head(p)], o_recv.at[t, p]).wait()

        return 0

    for t in range(4):
        out_self(t).wait()
    lax.fori_loop(0, RING, drain_out, 0)


def hand_over(*refs):
    ins, outs, held, load, store = refs[:4], refs[4:8], refs[8], refs[9], refs[10]
    half = BLK // 2

    def loads(n):
        rows = pl.ds(n % 2 * half, half)
        return pltpu.make_async_copy(ins[n // 2].at[rows, :], held.at[n], load.at[n])

    def stores(n):
        rows = pl.ds(n % 2 * half, half)
        return pltpu.make_async_copy(held.at[n], outs[n // 2].at[rows, :], store.at[n])

    for n in range(8):
        loads(n).start()
    for n in range(8):
        loads(n).wait()
        stores(n).start()
    for n in range(8):
        stores(n).wait()


def per_device(seqs, queries, keys, values, out_grad, event_bucket, slope, block_user, lengths):
    wide = jax.ShapeDtypeStruct((BLK, RING * HD), bf16)
    hbm = pl.BlockSpec(memory_space=pl.ANY)
    down = lambda n: pltpu.VMEM((n, BLK, HD), f32)
    across = lambda n: pltpu.VMEM((n, HD, BLK), f32)
    dma = pltpu.SemaphoreType.DMA
    results = pl.pallas_call(
        functools.partial(kernel, seqs),
        out_shape=(wide,) * 4,
        in_specs=[hbm] * 8,
        out_specs=(hbm,) * 4,
        scratch_shapes=[
            pltpu.SMEM((RING,), f32),
            pltpu.SMEM((seqs * RING,), i32),
            pltpu.SMEM(lengths.shape, i32),
            pltpu.VMEM((BLK,), i32),
            pltpu.VMEM((11, BLK, HD), bf16),
            pltpu.VMEM((12, BLK, HD), bf16),
            pltpu.VMEM((12, BLK, HD), bf16),
            pltpu.VMEM((11, BLK, HD), bf16),
            pltpu.VMEM((BLK, RING * HD), bf16),
            pltpu.VMEM((8, BLK), f32),
            pltpu.VMEM((8, 8, BLK), f32),
            pltpu.VMEM((8, 8, BLK), f32),
            down(12),
            pltpu.VMEM((11, 8, BLK), f32),
            pltpu.VMEM((8, 8, BLK), f32),
            down(8), down(8), across(8), across(8), down(8), down(8), across(11), across(11),
            pltpu.VMEM((4, 8, BLK, HD), bf16),
            pltpu.VMEM((2, 8, BLK, HD), bf16),
            pltpu.VMEM((2, 8, BLK, HD), bf16),
            dma, dma((4,)), dma((5,)), dma((4, 8)), dma((4, 8)), dma((8,)), dma((8,)), dma((3, 8)), dma((3, 8)),
            dma((2, 8)), dma((2, 8)), dma((4, 8)), dma((4, 8)), dma((4,)),
        ],
        compiler_params=pltpu.CompilerParams(
            collective_id=0, has_side_effects=True, vmem_limit_bytes=62 * 2**20),
        cost_estimate=pl.CostEstimate(
            flops=36 * 6 * 2 * BLK * BLK * HD, bytes_accessed=8 * BLK * RING * HD * 2, transcendentals=36 * BLK * BLK),
    )(slope, block_user, lengths, event_bucket, queries, keys, values, out_grad)
    return pl.pallas_call(
        hand_over,
        out_shape=(wide,) * 4,
        in_specs=[hbm] * 4,
        out_specs=(hbm,) * 4,
        scratch_shapes=[pltpu.VMEM((8, BLK // 2, RING * HD), bf16), dma((8,)), dma((8,))],
        compiler_params=pltpu.CompilerParams(vmem_limit_bytes=62 * 2**20),
    )(*results)


def solution(mesh):
    spread = P(("seq", "pair"), None)
    return jax.shard_map(
        functools.partial(per_device, mesh.shape["seq"]),
        mesh=mesh,
        in_specs=(spread, spread, spread, spread, P(("seq", "pair")), P(), P(), P()),
        out_specs=(spread,) * 4,
        check_vma=False,
    )
```

```python
import functools

import jax
import jax.numpy as jnp
from jax import lax
from jax.experimental import pallas as pl
from jax.experimental.pallas import tpu as pltpu
from jax.sharding import PartitionSpec as P

BLK = 256
HD = 128
RING = 8
MESH = pl.DeviceIdType.MESH
f32, bf16, i32 = jnp.float32, jnp.bfloat16, jnp.int32
SCALE = HD ** -0.5
NN = (((1,), (0,)), ((), ()))
NT = (((1,), (1,)), ((), ()))


def dot(a, b, dims=NN):
    return lax.dot_general(a, b, dims, preferred_element_type=f32)


def kernel(
    seqs, slope_hbm, user_hbm, length_hbm, bucket_hbm, q_hbm, k_hbm, v_hbm, g_hbm,
    o_out, dq_out, dk_out, dv_out,
    slope_ref, user_ref, length_ref, bucket_ref, QB, KB, VB, GB, G_own, B_own, B_ring, B_cross, colB, rowB, inv,
    OJ, QJ, VI, KI, FJU, FJW, FIU, FIW,
    stage, cross_out, cross_in,
    load_sem, small_sem, self_sem, in_send, in_recv, b_send, b_recv, x_send, x_recv, r_send, r_recv, o_send, o_recv, o_self,
):
    seq, pair = lax.axis_index("seq"), lax.axis_index("pair")
    blocks = seqs * RING
    y, core = pair // 2, pair % 2
    up, down = (seq + 1) % seqs, (seq + seqs - 1) % seqs
    outs = (o_out, dq_out, dk_out, dv_out)
    rings = (QB, KB, VB, GB)

    def offset(k):
        dy = jnp.where(k < 2, 0, jnp.where(k < 6, 1 + 2 * (k % 2), 2))
        dc = jnp.where(k < 2, k, jnp.where(k < 6, k // 4, k - 6))
        return dy, dc

    def place(k):
        dy, dc = offset(k)
        return ((y + dy) % 4) * 2 + (core + dc) % 2

    def source(k):
        dy, dc = offset(k)
        return ((y + 4 - dy) % 4) * 2 + (core + dc) % 2

    barrier = pltpu.get_barrier_semaphore()

    def greet(k, _):
        pl.semaphore_signal(barrier, inc=1, device_id=(seq, place(k)), device_id_type=MESH)
        return 0

    lax.fori_loop(1, RING, greet, 0)
    pl.semaphore_signal(barrier, inc=1, device_id=(up, pair), device_id_type=MESH)
    pl.semaphore_signal(barrier, inc=1, device_id=(down, pair), device_id_type=MESH)

    load = pltpu.make_async_copy(g_hbm, G_own, load_sem)
    load.start()
    smalls = [
        pltpu.make_async_copy(src, dst, small_sem.at[n])
        for n, (src, dst) in enumerate((
            (user_hbm, user_ref), (length_hbm, length_ref), (slope_hbm, slope_ref), (bucket_hbm, bucket_ref)))
    ]
    for small in smalls:
        small.start()
    for small in smalls:
        small.wait()

    def block_user(block):
        return user_ref[jnp.clip(block, 0, blocks - 1)]

    def live_rows(block):
        user = block_user(block)
        last = (block == blocks - 1) | (block_user(block + 1) != user)
        return jnp.where(last, lax.rem(length_ref[user] - 1, BLK) + 1, BLK)

    def prepare(p, _):
        zero = jnp.zeros((BLK, HD), f32)
        OJ[p] = zero
        QJ[p] = zero
        FJU[p] = zero
        FJW[p] = zero
        zero = jnp.zeros((HD, BLK), f32)
        VI[p] = zero
        KI[p] = zero
        FIU[p] = zero
        FIW[p] = zero

        @pl.when(p < 3)
        def _():
            FIU[8 + p] = zero
            FIW[8 + p] = zero

        length = length_ref[block_user(RING * seq + p)]
        inv[p] = 1.0 / jnp.full((8, BLK), length.astype(f32), f32)
        return 0

    lax.fori_loop(0, RING, prepare, 0)
    B_own[...] = jnp.broadcast_to(bucket_ref[...].astype(f32).reshape(1, BLK), (8, BLK))
    load.wait()
    own_live = live_rows(RING * seq + pair)

    def mask_own(n, _):
        rows = pl.ds(pl.multiple_of(n * 32, 32), 32)
        row = lax.broadcasted_iota(i32, (32, RING * HD), 0) + n * 32
        G_own[rows, :] = jnp.where(row < own_live, G_own[rows, :].astype(f32), 0.0).astype(bf16)
        return 0

    lax.fori_loop(0, BLK // 32, mask_own, 0)
    pl.semaphore_wait(barrier, RING + 1)

    sources = (q_hbm, k_hbm, v_hbm, G_own)

    def head(p):
        return pl.ds(pl.multiple_of(p * HD, HD), HD)

    def bucket_copy(k):
        return pltpu.make_async_remote_copy(
            B_own, B_ring.at[pair], b_send.at[k], b_recv.at[pair], device_id=(seq, place(k)), device_id_type=MESH)

    def in_copy(t, k):
        p = place(k)
        return pltpu.make_async_remote_copy(
            sources[t].at[:, head(p)], rings[t].at[pair], in_send.at[t, k], in_recv.at[t, pair],
            device_id=(seq, p), device_id_type=MESH)

    def self_copy(t):
        return pltpu.make_async_copy(sources[t].at[:, head(pair)], rings[t].at[pair], self_sem.at[t])

    for t in range(4):
        self_copy(t).start()
    self_bucket = pltpu.make_async_copy(B_own, B_ring.at[pair], self_sem.at[4])
    self_bucket.start()

    def send_order(first, second):
        def send(k, tensors):
            for t in tensors:
                in_copy(t, k).start()

        send(1, first + second)

        def near(target, tensors):
            k = 2 + 2 * ((target + core) % 2)
            send(k, tensors)
            send(k + 1, tensors)

        def far(target, tensors):
            send(6 + (target + core) % 2, tensors)

        near(0, first + second)
        far(0, first)
        near(1, first)
        far(1, first)
        far(0, second)
        near(1, second)
        far(1, second)

    def send_buckets(k, _):
        bucket_copy(k).start()
        return 0

    lax.fori_loop(1, RING, send_buckets, 0)

    @pl.when(pair >= 4)
    def _():
        send_order((1, 2), (0, 3))

    @pl.when(pair < 4)
    def _():
        send_order((0, 3), (1, 2))

    for t in range(4):
        self_copy(t).wait()
    self_bucket.wait()

    def wait_in(t, p):
        pltpu.make_async_copy(rings[t].at[p], rings[t].at[p], in_recv.at[t, p]).wait()

    def cross_copies(p, upward):
        if upward:
            pairs = ((KB.at[p], KB.at[p + 4]), (VB.at[p], VB.at[p + 4]), (B_ring.at[p], B_cross.at[p]))
            to = (up, pair)
        else:
            pairs = ((QB.at[p], QB.at[p + 8]), (GB.at[p], GB.at[p + 8]), (B_ring.at[p], B_cross.at[p]))
            to = (down, pair)
        return [
            pltpu.make_async_remote_copy(
                src, dst, x_send.at[n, p], x_recv.at[n, p], device_id=to, device_id_type=MESH)
            for n, (src, dst) in enumerate(pairs)
        ]

    def pass_on(k, _):
        p = source(k)

        @pl.when(k > 0)
        def _():
            pltpu.make_async_copy(B_ring.at[p], B_ring.at[p], b_recv.at[p]).wait()

        @pl.when(p >= 4)
        def _():
            @pl.when(k > 0)
            def _():
                wait_in(1, p)
                wait_in(2, p)

            for copy in cross_copies(p, True):
                copy.start()

        @pl.when(p < 4)
        def _():
            @pl.when(k > 0)
            def _():
                wait_in(0, p)
                wait_in(3, p)

            @pl.when(p < 3)
            def _():
                for copy in cross_copies(p, False):
                    copy.start()

        return 0


    half_slope = 0.5 * slope_ref[pair]

    def arrive(k):
        p = source(k)

        @pl.when(k > 0)
        def _():
            @pl.when(p >= 4)
            def _():
                wait_in(0, p)
                wait_in(3, p)

            @pl.when(p < 4)
            def _():
                wait_in(1, p)
                wait_in(2, p)

        row = B_ring[p] * half_slope
        rowB[p] = row
        colB[p] = jnp.broadcast_to(row[0:1], (HD, BLK)).T

        @pl.when(p >= 4)
        def _():
            for copy in cross_copies(p, True):
                copy.wait_recv()
            crossed = B_cross[p] * half_slope
            colB[p + 4] = jnp.broadcast_to(crossed[0:1], (HD, BLK)).T

        @pl.when(p < 3)
        def _():
            for copy in cross_copies(p, False):
                copy.wait_recv()
            rowB[p + 8] = B_cross[p] * half_slope

    def products(xj, yj, xi, yi):
        return dot(xj, xi, NT), dot(yj, yi, NT)

    def pointwise(raw, d_attn, column, row, weight, mask=None):
        half = raw * (0.5 * SCALE) - jnp.abs(jnp.concatenate([column, column], axis=1) - row)
        th = jnp.tanh(half)
        pw = th * weight + weight
        if mask is not None:
            pw = jnp.where(mask, pw, 0.0)
        aw = half * pw
        return aw.astype(bf16), (d_attn * (pw + aw * (1.0 - th))).astype(bf16)

    def spread(xj, yj, xi, yi, attn, score):
        return dot(attn, yi), dot(score, xi), dot(yj.T, attn), dot(xj.T, score)

    class Diagonal:
        def __init__(self, p):
            self.p = p
            self.operands = (QB[p], GB[p], KB[p], VB[p])

        def first(self):
            self.raw = products(*self.operands)

        def second(self):
            p = self.p
            mask = lax.broadcasted_iota(i32, (BLK, BLK), 0) >= lax.broadcasted_iota(i32, (BLK, BLK), 1)
            self.tiles = pointwise(*self.raw, colB[p], rowB[p][0:1], inv[p][0:1], mask)

        def third(self):
            p = self.p
            uj, wj, ui, wi = spread(*self.operands, *self.tiles)
            OJ[p] += uj
            QJ[p] += wj
            VI[p] += ui
            KI[p] += wi

    class Slot:
        def __init__(self, p, r):
            j, i = jnp.maximum(p, r), jnp.minimum(p, r)
            upper = j >= 4
            ja = jnp.where(upper, j + 4, j)
            ia = jnp.where(upper, i, i + 8)
            base = RING * seq
            user_i, user_j = block_user(base + i), block_user(base + j)
            inside = user_i == user_j
            below = (block_user(base + j - 8) == user_i) & (seq > 0)
            above = (block_user(base + i + 8) == user_j) & (seq < seqs - 1)
            flag = jnp.where(upper, below, above)
            valid = jnp.where(inside | flag, 1.0, 0.0)
            self.on = jnp.where(flag, 1.0, 0.0)
            self.weight = inv[jnp.where(upper, i, j)][0:1] * valid
            self.where = (j, i, ja, ia)

            def pick(a, b):
                return lax.select(flag, a, b)

            self.pick = pick
            self.operands = (pick(KB[ja], QB[j]), pick(VB[ja], GB[j]), pick(QB[ia], KB[i]), pick(GB[ia], VB[i]))

        def first(self):
            self.raw = products(*self.operands)

        def second(self):
            j, i, ja, ia = self.where
            self.tiles = pointwise(
                *self.raw, self.pick(colB[ja], colB[j]), self.pick(rowB[ia], rowB[i])[0:1], self.weight)

        def third(self):
            j, i, ja, ia = self.where
            on, off = self.on, 1.0 - self.on
            uj, wj, ui, wi = spread(*self.operands, *self.tiles)
            OJ[j] += uj * off
            QJ[j] += wj * off
            FJU[j] += uj * on
            FJW[j] += wj * on
            VI[i] += ui * off
            KI[i] += wi * off
            FIU[ia] += ui * on
            FIW[ia] += wi * on

    def together(*pairs):
        for pair_ in pairs:
            pair_.first()
        pairs[0].second()
        for n, pair_ in enumerate(pairs):
            if n + 1 < len(pairs):
                pairs[n + 1].second()
            pair_.third()

    back = 0.5 * SCALE

    def out_copy(t, p):
        return pltpu.make_async_remote_copy(
            stage.at[t, p], outs[t].at[:, head(pair)], o_send.at[t, p], o_recv.at[t, pair],
            device_id=(seq, p), device_id_type=MESH)

    def out_self(t):
        return pltpu.make_async_copy(stage.at[t, pair], outs[t].at[:, head(pair)], o_self.at[t])

    def emit(t, p):
        @pl.when(p != pair)
        def _():
            out_copy(t, p).start()

        @pl.when(p == pair)
        def _():
            out_self(t).start()

    def return_copies(p, downward):
        to = (down, pair) if downward else (up, pair)
        return [
            pltpu.make_async_remote_copy(
                cross_out.at[n, p], cross_in.at[n, p], r_send.at[n, p], r_recv.at[n, p],
                device_id=to, device_id_type=MESH)
            for n in range(2)
        ]

    def live_mask(p):
        return lax.broadcasted_iota(i32, (BLK, HD), 0) < live_rows(RING * seq + p)

    def finish(p):
        o = OJ[p] + FIU[p].T
        dq = (QJ[p] + FIW[p].T) * back
        dv = VI[p].T
        dk = KI[p].T * back

        @pl.when(p >= 4)
        def _():
            cross_out[0, p] = FJU[p].astype(bf16)
            cross_out[1, p] = (FJW[p] * back).astype(bf16)
            for copy in return_copies(p, True):
                copy.start()
            FJU[p] = dv
            FJW[p] = dk

        @pl.when(p < 3)
        def _():
            cross_out[0, p] = FIU[p + 8].T.astype(bf16)
            cross_out[1, p] = (FIW[p + 8].T * back).astype(bf16)
            for copy in return_copies(p, False):
                copy.start()
            OJ[p] = o
            QJ[p] = dq

        @pl.when(p >= 3)
        def _():
            stage[0, p] = jnp.where(live_mask(p), o, 0.0).astype(bf16)
            stage[1, p] = dq.astype(bf16)
            emit(0, p)
            emit(1, p)

        @pl.when(p < 4)
        def _():
            stage[2, p] = (dk + FJW[p] * back).astype(bf16)
            stage[3, p] = (dv + FJU[p]).astype(bf16)
            emit(2, p)
            emit(3, p)

    def step(k, _):
        arrive(k)
        p = source(k)

        def two(m, _):
            together(Slot(p, source(2 * m)), Slot(p, source(2 * m + 1)))
            return 0

        lax.fori_loop(0, k // 2, two, 0)

        @pl.when(k % 2 == 1)
        def _():
            together(Slot(p, source(k - 1)), Diagonal(p))

        @pl.when(k % 2 == 0)
        def _():
            together(Diagonal(p))

        return 0

    def advance(k, _):
        first = jnp.where(k == 0, 0, jnp.where(k == 2, 2, 6))
        end = jnp.where(k == 0, 2, jnp.where(k == 2, 6 + 2 * core, jnp.where(k == 4, 8 - 2 * core, 6)))
        lax.fori_loop(first, end, pass_on, 0)
        step(k, 0)
        return 0

    lax.fori_loop(0, RING - 1, advance, 0)
    arrive(RING - 1)
    last = source(RING - 1)

    def turn(m):
        return source(jnp.where(m < 5, m + 2, 6 - m))

    def last_two(m, _):
        one, two = turn(2 * m), turn(2 * m + 1)
        together(Slot(last, one), Slot(last, two))
        finish(one)
        finish(two)
        return 0

    lax.fori_loop(0, 3, last_two, 0)
    together(Slot(last, turn(6)), Diagonal(last))
    finish(last)
    finish(turn(6))

    def drain_in(k, _):
        p = source(k)

        @pl.when(p >= 4)
        def _():
            for copy in cross_copies(p, True):
                copy.wait_send()

        @pl.when(p < 3)
        def _():
            for copy in cross_copies(p, False):
                copy.wait_send()

        @pl.when(k > 0)
        def _():
            bucket_copy(k).wait_send()
            for t in range(4):
                in_copy(t, k).wait_send()

        return 0


    def settle(k, _):
        p = source((k + 2) % RING)

        @pl.when(p >= 4)
        def _():
            for copy in return_copies(p, True):
                copy.wait_recv()
            stage[2, p] = (FJW[p] + cross_in[1, p].astype(f32)).astype(bf16)
            stage[3, p] = (FJU[p] + cross_in[0, p].astype(f32)).astype(bf16)
            emit(2, p)
            emit(3, p)

        @pl.when(p < 3)
        def _():
            for copy in return_copies(p, False):
                copy.wait_recv()
            stage[0, p] = jnp.where(live_mask(p), OJ[p] + cross_in[0, p].astype(f32), 0.0).astype(bf16)
            stage[1, p] = (QJ[p] + cross_in[1, p].astype(f32)).astype(bf16)
            emit(0, p)
            emit(1, p)

        return 0

    lax.fori_loop(0, RING, settle, 0)
    lax.fori_loop(0, RING, drain_in, 0)

    def drain_out(k, _):
        p = source(k)

        @pl.when(p >= 4)
        def _():
            for copy in return_copies(p, True):
                copy.wait_send()

        @pl.when(p < 3)
        def _():
            for copy in return_copies(p, False):
                copy.wait_send()

        @pl.when(k > 0)
        def _():
            for t in range(4):
                out_copy(t, p).wait_send()
                pltpu.make_async_copy(stage.at[t, p], outs[t].at[:, head(p)], o_recv.at[t, p]).wait()

        return 0

    for t in range(4):
        out_self(t).wait()
    lax.fori_loop(0, RING, drain_out, 0)


def hand_over(*refs):
    ins, outs, held, load, store = refs[:4], refs[4:8], refs[8], refs[9], refs[10]
    half = BLK // 2

    def loads(n):
        rows = pl.ds(n % 2 * half, half)
        return pltpu.make_async_copy(ins[n // 2].at[rows, :], held.at[n], load.at[n])

    def stores(n):
        rows = pl.ds(n % 2 * half, half)
        return pltpu.make_async_copy(held.at[n], outs[n // 2].at[rows, :], store.at[n])

    for n in range(8):
        loads(n).start()
    for n in range(8):
        loads(n).wait()
        stores(n).start()
    for n in range(8):
        stores(n).wait()


def per_device(seqs, queries, keys, values, out_grad, event_bucket, slope, block_user, lengths):
    wide = jax.ShapeDtypeStruct((BLK, RING * HD), bf16)
    hbm = pl.BlockSpec(memory_space=pl.ANY)
    down = lambda n: pltpu.VMEM((n, BLK, HD), f32)
    across = lambda n: pltpu.VMEM((n, HD, BLK), f32)
    dma = pltpu.SemaphoreType.DMA
    results = pl.pallas_call(
        functools.partial(kernel, seqs),
        out_shape=(wide,) * 4,
        in_specs=[hbm] * 8,
        out_specs=(hbm,) * 4,
        scratch_shapes=[
            pltpu.SMEM((RING,), f32),
            pltpu.SMEM((seqs * RING,), i32),
            pltpu.SMEM(lengths.shape, i32),
            pltpu.VMEM((BLK,), i32),
            pltpu.VMEM((11, BLK, HD), bf16),
            pltpu.VMEM((12, BLK, HD), bf16),
            pltpu.VMEM((12, BLK, HD), bf16),
            pltpu.VMEM((11, BLK, HD), bf16),
            pltpu.VMEM((BLK, RING * HD), bf16),
            pltpu.VMEM((8, BLK), f32),
            pltpu.VMEM((8, 8, BLK), f32),
            pltpu.VMEM((8, 8, BLK), f32),
            down(12),
            pltpu.VMEM((11, 8, BLK), f32),
            pltpu.VMEM((8, 8, BLK), f32),
            down(8), down(8), across(8), across(8), down(8), down(8), across(11), across(11),
            pltpu.VMEM((4, 8, BLK, HD), bf16),
            pltpu.VMEM((2, 8, BLK, HD), bf16),
            pltpu.VMEM((2, 8, BLK, HD), bf16),
            dma, dma((4,)), dma((5,)), dma((4, 8)), dma((4, 8)), dma((8,)), dma((8,)), dma((3, 8)), dma((3, 8)),
            dma((2, 8)), dma((2, 8)), dma((4, 8)), dma((4, 8)), dma((4,)),
        ],
        compiler_params=pltpu.CompilerParams(
            collective_id=0, has_side_effects=True, vmem_limit_bytes=62 * 2**20),
        cost_estimate=pl.CostEstimate(
            flops=36 * 6 * 2 * BLK * BLK * HD, bytes_accessed=8 * BLK * RING * HD * 2, transcendentals=36 * BLK * BLK),
    )(slope, block_user, lengths, event_bucket, queries, keys, values, out_grad)
    return pl.pallas_call(
        hand_over,
        out_shape=(wide,) * 4,
        in_specs=[hbm] * 4,
        out_specs=(hbm,) * 4,
        scratch_shapes=[pltpu.VMEM((8, BLK // 2, RING * HD), bf16), dma((8,)), dma((8,))],
        compiler_params=pltpu.CompilerParams(vmem_limit_bytes=62 * 2**20),
    )(*results)


def solution(mesh):
    spread = P(("seq", "pair"), None)
    return jax.shard_map(
        functools.partial(per_device, mesh.shape["seq"]),
        mesh=mesh,
        in_specs=(spread, spread, spread, spread, P(("seq", "pair")), P(), P(), P()),
        out_specs=(spread,) * 4,
        check_vma=False,
    )
```

```python
import functools

import jax
import jax.numpy as jnp
from jax import lax
from jax.experimental import pallas as pl
from jax.experimental.pallas import tpu as pltpu
from jax.sharding import PartitionSpec as P

BLK = 256
HD = 128
RING = 8
MESH = pl.DeviceIdType.MESH
f32, bf16, i32 = jnp.float32, jnp.bfloat16, jnp.int32
SCALE = HD ** -0.5
NN = (((1,), (0,)), ((), ()))
NT = (((1,), (1,)), ((), ()))


def dot(a, b, dims=NN):
    return lax.dot_general(a, b, dims, preferred_element_type=f32)


def kernel(
    seqs, slope_hbm, user_hbm, length_hbm, bucket_hbm, q_hbm, k_hbm, v_hbm, g_hbm,
    o_out, dq_out, dk_out, dv_out,
    slope_ref, user_ref, length_ref, bucket_ref, QB, KB, VB, GB, G_own, B_own, B_ring, B_cross, colB, rowB, inv,
    OJ, QJ, VI, KI, FJU, FJW, FIU, FIW,
    stage, cross_out, cross_in,
    load_sem, small_sem, self_sem, in_send, in_recv, b_send, b_recv, x_send, x_recv, r_send, r_recv, o_send, o_recv, o_self,
):
    seq, pair = lax.axis_index("seq"), lax.axis_index("pair")
    blocks = seqs * RING
    y, core = pair // 2, pair % 2
    up, down = (seq + 1) % seqs, (seq + seqs - 1) % seqs
    has_up, has_down = seq < seqs - 1, seq > 0
    outs = (o_out, dq_out, dk_out, dv_out)
    rings = (QB, KB, VB, GB)

    def offset(k):
        dy = jnp.where(k < 2, 0, jnp.where(k < 6, 1 + 2 * (k % 2), 2))
        dc = jnp.where(k < 2, k, jnp.where(k < 6, k // 4, k - 6))
        return dy, dc

    def place(k):
        dy, dc = offset(k)
        return ((y + dy) % 4) * 2 + (core + dc) % 2

    def source(k):
        dy, dc = offset(k)
        return ((y + 4 - dy) % 4) * 2 + (core + dc) % 2

    barrier = pltpu.get_barrier_semaphore()

    def greet(k, _):
        pl.semaphore_signal(barrier, inc=1, device_id=(seq, place(k)), device_id_type=MESH)
        return 0

    lax.fori_loop(1, RING, greet, 0)

    @pl.when(has_up)
    def _():
        pl.semaphore_signal(barrier, inc=1, device_id=(up, pair), device_id_type=MESH)

    @pl.when(has_down)
    def _():
        pl.semaphore_signal(barrier, inc=1, device_id=(down, pair), device_id_type=MESH)


    load = pltpu.make_async_copy(g_hbm, G_own, load_sem)
    load.start()
    smalls = [
        pltpu.make_async_copy(src, dst, small_sem.at[n])
        for n, (src, dst) in enumerate((
            (user_hbm, user_ref), (length_hbm, length_ref), (slope_hbm, slope_ref), (bucket_hbm, bucket_ref)))
    ]
    for small in smalls:
        small.start()
    for small in smalls:
        small.wait()

    def block_user(block):
        return user_ref[jnp.clip(block, 0, blocks - 1)]

    def live_rows(block):
        user = block_user(block)
        last = (block == blocks - 1) | (block_user(block + 1) != user)
        return jnp.where(last, lax.rem(length_ref[user] - 1, BLK) + 1, BLK)

    def prepare(p, _):
        zero = jnp.zeros((BLK, HD), f32)
        OJ[p] = zero
        QJ[p] = zero
        FJU[p] = zero
        FJW[p] = zero
        zero = jnp.zeros((HD, BLK), f32)
        VI[p] = zero
        KI[p] = zero
        FIU[p] = zero
        FIW[p] = zero

        @pl.when(p < 3)
        def _():
            FIU[8 + p] = zero
            FIW[8 + p] = zero

        @pl.when((p >= 4) & (seq == 0))
        def _():
            KB[p + 4] = jnp.zeros((BLK, HD), bf16)
            VB[p + 4] = jnp.zeros((BLK, HD), bf16)
            colB[p + 4] = jnp.zeros((BLK, HD), f32)

        @pl.when((p < 3) & (seq == 0))
        def _():
            cross_in[0, p] = jnp.zeros((BLK, HD), bf16)
            cross_in[1, p] = jnp.zeros((BLK, HD), bf16)

        @pl.when((p < 3) & (seq == seqs - 1))
        def _():
            QB[p + 8] = jnp.zeros((BLK, HD), bf16)
            GB[p + 8] = jnp.zeros((BLK, HD), bf16)
            rowB[p + 8] = jnp.zeros((8, BLK), f32)

        @pl.when((p >= 4) & (seq == seqs - 1))
        def _():
            cross_in[0, p] = jnp.zeros((BLK, HD), bf16)
            cross_in[1, p] = jnp.zeros((BLK, HD), bf16)

        length = length_ref[block_user(RING * seq + p)]
        inv[p] = 1.0 / jnp.full((8, BLK), length.astype(f32), f32)
        return 0

    lax.fori_loop(0, RING, prepare, 0)
    B_own[...] = jnp.broadcast_to(bucket_ref[...].astype(f32).reshape(1, BLK), (8, BLK))
    load.wait()
    own_live = live_rows(RING * seq + pair)

    def mask_own(n, _):
        rows = pl.ds(pl.multiple_of(n * 32, 32), 32)
        row = lax.broadcasted_iota(i32, (32, RING * HD), 0) + n * 32
        G_own[rows, :] = jnp.where(row < own_live, G_own[rows, :].astype(f32), 0.0).astype(bf16)
        return 0

    lax.fori_loop(0, BLK // 32, mask_own, 0)
    pl.semaphore_wait(barrier, RING - 1 + jnp.where(has_up, 1, 0) + jnp.where(has_down, 1, 0))

    sources = (q_hbm, k_hbm, v_hbm, G_own)

    def head(p):
        return pl.ds(pl.multiple_of(p * HD, HD), HD)

    def bucket_copy(k):
        return pltpu.make_async_remote_copy(
            B_own, B_ring.at[pair], b_send.at[k], b_recv.at[pair], device_id=(seq, place(k)), device_id_type=MESH)

    def in_copy(t, k):
        p = place(k)
        return pltpu.make_async_remote_copy(
            sources[t].at[:, head(p)], rings[t].at[pair], in_send.at[t, k], in_recv.at[t, pair],
            device_id=(seq, p), device_id_type=MESH)

    def self_copy(t):
        return pltpu.make_async_copy(sources[t].at[:, head(pair)], rings[t].at[pair], self_sem.at[t])

    for t in range(4):
        self_copy(t).start()
    self_bucket = pltpu.make_async_copy(B_own, B_ring.at[pair], self_sem.at[4])
    self_bucket.start()

    def send_order(first, second):
        def send(k, tensors):
            for t in tensors:
                in_copy(t, k).start()

        send(1, first + second)

        def near(target, tensors):
            k = 2 + 2 * ((target + core) % 2)
            send(k, tensors)
            send(k + 1, tensors)

        def far(target, tensors):
            send(6 + (target + core) % 2, tensors)

        near(0, first + second)
        far(0, first)
        near(1, first)
        far(1, first)
        far(0, second)
        near(1, second)
        far(1, second)

    def send_buckets(k, _):
        bucket_copy(k).start()
        return 0

    lax.fori_loop(1, RING, send_buckets, 0)

    @pl.when(pair >= 4)
    def _():
        send_order((1, 2), (0, 3))

    @pl.when(pair < 4)
    def _():
        send_order((0, 3), (1, 2))

    for t in range(4):
        self_copy(t).wait()
    self_bucket.wait()

    def wait_in(t, p):
        pltpu.make_async_copy(rings[t].at[p], rings[t].at[p], in_recv.at[t, p]).wait()

    def cross_copies(p, upward):
        if upward:
            pairs = ((KB.at[p], KB.at[p + 4]), (VB.at[p], VB.at[p + 4]), (B_ring.at[p], B_cross.at[p]))
            to = (up, pair)
        else:
            pairs = ((QB.at[p], QB.at[p + 8]), (GB.at[p], GB.at[p + 8]), (B_ring.at[p], B_cross.at[p]))
            to = (down, pair)
        return [
            pltpu.make_async_remote_copy(
                src, dst, x_send.at[n, p], x_recv.at[n, p], device_id=to, device_id_type=MESH)
            for n, (src, dst) in enumerate(pairs)
        ]

    def pass_on(k, _):
        p = source(k)

        @pl.when(k > 0)
        def _():
            pltpu.make_async_copy(B_ring.at[p], B_ring.at[p], b_recv.at[p]).wait()

        @pl.when(p >= 4)
        def _():
            @pl.when(k > 0)
            def _():
                wait_in(1, p)
                wait_in(2, p)

            @pl.when(has_up)
            def _():
                for copy in cross_copies(p, True):
                    copy.start()

        @pl.when(p < 4)
        def _():
            @pl.when(k > 0)
            def _():
                wait_in(0, p)
                wait_in(3, p)

            @pl.when((p < 3) & has_down)
            def _():
                for copy in cross_copies(p, False):
                    copy.start()

        return 0


    half_slope = 0.5 * slope_ref[pair]

    def arrive(k):
        p = source(k)

        @pl.when(k > 0)
        def _():
            @pl.when(p >= 4)
            def _():
                wait_in(0, p)
                wait_in(3, p)

            @pl.when(p < 4)
            def _():
                wait_in(1, p)
                wait_in(2, p)

        row = B_ring[p] * half_slope
        rowB[p] = row
        colB[p] = jnp.broadcast_to(row[0:1], (HD, BLK)).T

        @pl.when((p >= 4) & has_down)
        def _():
            for copy in cross_copies(p, True):
                copy.wait_recv()
            crossed = B_cross[p] * half_slope
            colB[p + 4] = jnp.broadcast_to(crossed[0:1], (HD, BLK)).T

        @pl.when((p < 3) & has_up)
        def _():
            for copy in cross_copies(p, False):
                copy.wait_recv()
            rowB[p + 8] = B_cross[p] * half_slope

    def products(xj, yj, xi, yi):
        return dot(xj, xi, NT), dot(yj, yi, NT)

    def pointwise(raw, d_attn, column, row, weight, mask=None):
        half = raw * (0.5 * SCALE) - jnp.abs(jnp.concatenate([column, column], axis=1) - row)
        th = jnp.tanh(half)
        pw = th * weight + weight
        if mask is not None:
            pw = jnp.where(mask, pw, 0.0)
        aw = half * pw
        return aw.astype(bf16), (d_attn * (pw + aw * (1.0 - th))).astype(bf16)

    def spread(xj, yj, xi, yi, attn, score):
        return dot(attn, yi), dot(score, xi), dot(yj.T, attn), dot(xj.T, score)

    class Diagonal:
        def __init__(self, p):
            self.p = p
            self.operands = (QB[p], GB[p], KB[p], VB[p])

        def first(self):
            self.raw = products(*self.operands)

        def second(self):
            p = self.p
            mask = lax.broadcasted_iota(i32, (BLK, BLK), 0) >= lax.broadcasted_iota(i32, (BLK, BLK), 1)
            self.tiles = pointwise(*self.raw, colB[p], rowB[p][0:1], inv[p][0:1], mask)

        def third(self):
            p = self.p
            uj, wj, ui, wi = spread(*self.operands, *self.tiles)
            OJ[p] += uj
            QJ[p] += wj
            VI[p] += ui
            KI[p] += wi

    class Slot:
        def __init__(self, p, r):
            j, i = jnp.maximum(p, r), jnp.minimum(p, r)
            upper = j >= 4
            ja = jnp.where(upper, j + 4, j)
            ia = jnp.where(upper, i, i + 8)
            base = RING * seq
            user_i, user_j = block_user(base + i), block_user(base + j)
            inside = user_i == user_j
            below = (block_user(base + j - 8) == user_i) & (seq > 0)
            above = (block_user(base + i + 8) == user_j) & (seq < seqs - 1)
            flag = jnp.where(upper, below, above)
            valid = jnp.where(inside | flag, 1.0, 0.0)
            self.on = jnp.where(flag, 1.0, 0.0)
            self.weight = inv[jnp.where(upper, i, j)][0:1] * valid
            self.where = (j, i, ja, ia)

            def pick(a, b):
                return lax.select(flag, a, b)

            self.pick = pick
            self.operands = (pick(KB[ja], QB[j]), pick(VB[ja], GB[j]), pick(QB[ia], KB[i]), pick(GB[ia], VB[i]))

        def first(self):
            self.raw = products(*self.operands)

        def second(self):
            j, i, ja, ia = self.where
            self.tiles = pointwise(
                *self.raw, self.pick(colB[ja], colB[j]), self.pick(rowB[ia], rowB[i])[0:1], self.weight)

        def third(self):
            j, i, ja, ia = self.where
            on, off = self.on, 1.0 - self.on
            uj, wj, ui, wi = spread(*self.operands, *self.tiles)
            OJ[j] += uj * off
            QJ[j] += wj * off
            FJU[j] += uj * on
            FJW[j] += wj * on
            VI[i] += ui * off
            KI[i] += wi * off
            FIU[ia] += ui * on
            FIW[ia] += wi * on

    def together(*tiles):
        count = len(tiles)
        tiles[0].first()
        for n in range(count + 1):
            if n + 1 < count:
                tiles[n + 1].first()
            if n < count:
                tiles[n].second()
            if n >= 1:
                tiles[n - 1].third()

    back = 0.5 * SCALE

    def out_copy(t, p):
        return pltpu.make_async_remote_copy(
            stage.at[t, p], outs[t].at[:, head(pair)], o_send.at[t, p], o_recv.at[t, pair],
            device_id=(seq, p), device_id_type=MESH)

    def out_self(t):
        return pltpu.make_async_copy(stage.at[t, pair], outs[t].at[:, head(pair)], o_self.at[t])

    def emit(t, p):
        @pl.when(p != pair)
        def _():
            out_copy(t, p).start()

        @pl.when(p == pair)
        def _():
            out_self(t).start()

    def return_copies(p, downward):
        to = (down, pair) if downward else (up, pair)
        return [
            pltpu.make_async_remote_copy(
                cross_out.at[n, p], cross_in.at[n, p], r_send.at[n, p], r_recv.at[n, p],
                device_id=to, device_id_type=MESH)
            for n in range(2)
        ]

    def live_mask(p):
        return lax.broadcasted_iota(i32, (BLK, HD), 0) < live_rows(RING * seq + p)

    def finish(p):
        o = OJ[p] + FIU[p].T
        dq = (QJ[p] + FIW[p].T) * back
        dv = VI[p].T
        dk = KI[p].T * back

        @pl.when(p >= 4)
        def _():
            cross_out[0, p] = FJU[p].astype(bf16)
            cross_out[1, p] = (FJW[p] * back).astype(bf16)

            @pl.when(has_down)
            def _():
                for copy in return_copies(p, True):
                    copy.start()

            FJU[p] = dv
            FJW[p] = dk

        @pl.when(p < 3)
        def _():
            cross_out[0, p] = FIU[p + 8].T.astype(bf16)
            cross_out[1, p] = (FIW[p + 8].T * back).astype(bf16)

            @pl.when(has_up)
            def _():
                for copy in return_copies(p, False):
                    copy.start()

            OJ[p] = o
            QJ[p] = dq

        @pl.when(p >= 3)
        def _():
            stage[0, p] = jnp.where(live_mask(p), o, 0.0).astype(bf16)
            stage[1, p] = dq.astype(bf16)
            emit(0, p)
            emit(1, p)

        @pl.when(p < 4)
        def _():
            stage[2, p] = (dk + FJW[p] * back).astype(bf16)
            stage[3, p] = (dv + FJU[p]).astype(bf16)
            emit(2, p)
            emit(3, p)

    def step(k, _):
        arrive(k)
        p = source(k)

        def four(m, _):
            together(*[Slot(p, source(4 * m + n)) for n in range(4)])
            return 0

        lax.fori_loop(0, k // 4, four, 0)
        rest = k - k % 4

        @pl.when(k % 4 == 0)
        def _():
            together(Diagonal(p))

        @pl.when(k % 4 == 1)
        def _():
            together(Slot(p, source(rest)), Diagonal(p))

        @pl.when(k % 4 == 2)
        def _():
            together(Slot(p, source(rest)), Slot(p, source(rest + 1)), Diagonal(p))

        @pl.when(k % 4 == 3)
        def _():
            together(*[Slot(p, source(rest + n)) for n in range(3)], Diagonal(p))

        return 0

    def advance(k, _):
        first = jnp.where(k == 0, 0, jnp.where(k == 2, 2, 6))
        end = jnp.where(k == 0, 2, jnp.where(k == 2, 6 + 2 * core, jnp.where(k == 4, 8 - 2 * core, 6)))
        lax.fori_loop(first, end, pass_on, 0)
        step(k, 0)
        return 0

    lax.fori_loop(0, RING - 1, advance, 0)
    arrive(RING - 1)
    last = source(RING - 1)

    def turn(m):
        return source(jnp.where(m < 5, m + 2, 6 - m))

    def last_two(m, _):
        one, two = turn(2 * m), turn(2 * m + 1)
        together(Slot(last, one), Slot(last, two))
        finish(one)
        finish(two)
        return 0

    lax.fori_loop(0, 3, last_two, 0)
    together(Slot(last, turn(6)), Diagonal(last))
    finish(last)
    finish(turn(6))

    def drain_in(k, _):
        p = source(k)

        @pl.when((p >= 4) & has_up)
        def _():
            for copy in cross_copies(p, True):
                copy.wait_send()

        @pl.when((p < 3) & has_down)
        def _():
            for copy in cross_copies(p, False):
                copy.wait_send()

        @pl.when(k > 0)
        def _():
            bucket_copy(k).wait_send()
            for t in range(4):
                in_copy(t, k).wait_send()

        return 0


    def settle(k, _):
        p = source((k + 2) % RING)

        @pl.when(p >= 4)
        def _():
            @pl.when(has_up)
            def _():
                for copy in return_copies(p, True):
                    copy.wait_recv()

            stage[2, p] = (FJW[p] + cross_in[1, p].astype(f32)).astype(bf16)
            stage[3, p] = (FJU[p] + cross_in[0, p].astype(f32)).astype(bf16)
            emit(2, p)
            emit(3, p)

        @pl.when(p < 3)
        def _():
            @pl.when(has_down)
            def _():
                for copy in return_copies(p, False):
                    copy.wait_recv()

            stage[0, p] = jnp.where(live_mask(p), OJ[p] + cross_in[0, p].astype(f32), 0.0).astype(bf16)
            stage[1, p] = (QJ[p] + cross_in[1, p].astype(f32)).astype(bf16)
            emit(0, p)
            emit(1, p)

        return 0

    lax.fori_loop(0, RING, settle, 0)
    lax.fori_loop(0, RING, drain_in, 0)

    def drain_out(k, _):
        p = source(k)

        @pl.when((p >= 4) & has_down)
        def _():
            for copy in return_copies(p, True):
                copy.wait_send()

        @pl.when((p < 3) & has_up)
        def _():
            for copy in return_copies(p, False):
                copy.wait_send()

        @pl.when(k > 0)
        def _():
            for t in range(4):
                out_copy(t, p).wait_send()
                pltpu.make_async_copy(stage.at[t, p], outs[t].at[:, head(p)], o_recv.at[t, p]).wait()

        return 0

    for t in range(4):
        out_self(t).wait()
    lax.fori_loop(0, RING, drain_out, 0)


def hand_over(*refs):
    ins, outs, held, load, store = refs[:4], refs[4:8], refs[8], refs[9], refs[10]
    half = BLK // 2

    def loads(n):
        rows = pl.ds(n % 2 * half, half)
        return pltpu.make_async_copy(ins[n // 2].at[rows, :], held.at[n], load.at[n])

    def stores(n):
        rows = pl.ds(n % 2 * half, half)
        return pltpu.make_async_copy(held.at[n], outs[n // 2].at[rows, :], store.at[n])

    for n in range(8):
        loads(n).start()
    for n in range(8):
        loads(n).wait()
        stores(n).start()
    for n in range(8):
        stores(n).wait()


def per_device(seqs, queries, keys, values, out_grad, event_bucket, slope, block_user, lengths):
    wide = jax.ShapeDtypeStruct((BLK, RING * HD), bf16)
    hbm = pl.BlockSpec(memory_space=pl.ANY)
    down = lambda n: pltpu.VMEM((n, BLK, HD), f32)
    across = lambda n: pltpu.VMEM((n, HD, BLK), f32)
    dma = pltpu.SemaphoreType.DMA
    results = pl.pallas_call(
        functools.partial(kernel, seqs),
        out_shape=(wide,) * 4,
        in_specs=[hbm] * 8,
        out_specs=(hbm,) * 4,
        scratch_shapes=[
            pltpu.SMEM((RING,), f32),
            pltpu.SMEM((seqs * RING,), i32),
            pltpu.SMEM(lengths.shape, i32),
            pltpu.VMEM((BLK,), i32),
            pltpu.VMEM((11, BLK, HD), bf16),
            pltpu.VMEM((12, BLK, HD), bf16),
            pltpu.VMEM((12, BLK, HD), bf16),
            pltpu.VMEM((11, BLK, HD), bf16),
            pltpu.VMEM((BLK, RING * HD), bf16),
            pltpu.VMEM((8, BLK), f32),
            pltpu.VMEM((8, 8, BLK), f32),
            pltpu.VMEM((8, 8, BLK), f32),
            down(12),
            pltpu.VMEM((11, 8, BLK), f32),
            pltpu.VMEM((8, 8, BLK), f32),
            down(8), down(8), across(8), across(8), down(8), down(8), across(11), across(11),
            pltpu.VMEM((4, 8, BLK, HD), bf16),
            pltpu.VMEM((2, 8, BLK, HD), bf16),
            pltpu.VMEM((2, 8, BLK, HD), bf16),
            dma, dma((4,)), dma((5,)), dma((4, 8)), dma((4, 8)), dma((8,)), dma((8,)), dma((3, 8)), dma((3, 8)),
            dma((2, 8)), dma((2, 8)), dma((4, 8)), dma((4, 8)), dma((4,)),
        ],
        compiler_params=pltpu.CompilerParams(
            collective_id=0, has_side_effects=True, vmem_limit_bytes=62 * 2**20),
        cost_estimate=pl.CostEstimate(
            flops=36 * 6 * 2 * BLK * BLK * HD, bytes_accessed=8 * BLK * RING * HD * 2, transcendentals=36 * BLK * BLK),
    )(slope, block_user, lengths, event_bucket, queries, keys, values, out_grad)
    return pl.pallas_call(
        hand_over,
        out_shape=(wide,) * 4,
        in_specs=[hbm] * 4,
        out_specs=(hbm,) * 4,
        scratch_shapes=[pltpu.VMEM((8, BLK // 2, RING * HD), bf16), dma((8,)), dma((8,))],
        compiler_params=pltpu.CompilerParams(vmem_limit_bytes=62 * 2**20),
    )(*results)


def solution(mesh):
    spread = P(("seq", "pair"), None)
    return jax.shard_map(
        functools.partial(per_device, mesh.shape["seq"]),
        mesh=mesh,
        in_specs=(spread, spread, spread, spread, P(("seq", "pair")), P(), P(), P()),
        out_specs=(spread,) * 4,
        check_vma=False,
    )
```

```python
import functools

import jax
import jax.numpy as jnp
from jax import lax
from jax.experimental import pallas as pl
from jax.experimental.pallas import tpu as pltpu
from jax.sharding import PartitionSpec as P

BLK = 256
HD = 128
RING = 8
MESH = pl.DeviceIdType.MESH
f32, bf16, i32 = jnp.float32, jnp.bfloat16, jnp.int32
SCALE = HD ** -0.5
NN = (((1,), (0,)), ((), ()))
NT = (((1,), (1,)), ((), ()))


def dot(a, b, dims=NN):
    return lax.dot_general(a, b, dims, preferred_element_type=f32)


def kernel(
    seqs, slope_hbm, user_hbm, length_hbm, bucket_hbm, q_hbm, k_hbm, v_hbm, g_hbm,
    o_out, dq_out, dk_out, dv_out,
    slope_ref, user_ref, length_ref, bucket_ref, QB, KB, VB, GB, G_own, B_own, B_ring, B_cross, colB, rowB, inv,
    OJ, QJ, VI, KI, FJU, FJW, FIU, FIW,
    stage, cross_out, cross_in,
    load_sem, small_sem, self_sem, in_send, in_recv, b_send, b_recv, x_send, x_recv, r_send, r_recv, o_send, o_recv, o_self,
):
    seq, pair = lax.axis_index("seq"), lax.axis_index("pair")
    blocks = seqs * RING
    y, core = pair // 2, pair % 2
    up, down = (seq + 1) % seqs, (seq + seqs - 1) % seqs
    has_up, has_down = seq < seqs - 1, seq > 0
    outs = (o_out, dq_out, dk_out, dv_out)
    rings = (QB, KB, VB, GB)

    def offset(k):
        dy = jnp.where(k < 2, 0, jnp.where(k < 6, 1 + 2 * (k % 2), 2))
        dc = jnp.where(k < 2, k, jnp.where(k < 6, k // 4, k - 6))
        return dy, dc

    def place(k):
        dy, dc = offset(k)
        return ((y + dy) % 4) * 2 + (core + dc) % 2

    def source(k):
        dy, dc = offset(k)
        return ((y + 4 - dy) % 4) * 2 + (core + dc) % 2

    barrier = pltpu.get_barrier_semaphore()

    def greet(k, _):
        pl.semaphore_signal(barrier, inc=1, device_id=(seq, place(k)), device_id_type=MESH)
        return 0

    lax.fori_loop(1, RING, greet, 0)

    @pl.when(has_up)
    def _():
        pl.semaphore_signal(barrier, inc=1, device_id=(up, pair), device_id_type=MESH)

    @pl.when(has_down)
    def _():
        pl.semaphore_signal(barrier, inc=1, device_id=(down, pair), device_id_type=MESH)


    load = pltpu.make_async_copy(g_hbm, G_own, load_sem)
    load.start()
    smalls = [
        pltpu.make_async_copy(src, dst, small_sem.at[n])
        for n, (src, dst) in enumerate((
            (user_hbm, user_ref), (length_hbm, length_ref), (slope_hbm, slope_ref), (bucket_hbm, bucket_ref)))
    ]
    for small in smalls:
        small.start()
    for small in smalls:
        small.wait()

    def block_user(block):
        return user_ref[jnp.clip(block, 0, blocks - 1)]

    def live_rows(block):
        user = block_user(block)
        last = (block == blocks - 1) | (block_user(block + 1) != user)
        return jnp.where(last, lax.rem(length_ref[user] - 1, BLK) + 1, BLK)

    def prepare(p, _):
        zero = jnp.zeros((BLK, HD), f32)
        OJ[p] = zero
        QJ[p] = zero
        FJU[p] = zero
        FJW[p] = zero
        zero = jnp.zeros((HD, BLK), f32)
        VI[p] = zero
        KI[p] = zero
        FIU[p] = zero
        FIW[p] = zero

        @pl.when(p < 3)
        def _():
            FIU[8 + p] = zero
            FIW[8 + p] = zero

        @pl.when((p >= 4) & (seq == 0))
        def _():
            KB[p + 4] = jnp.zeros((BLK, HD), bf16)
            VB[p + 4] = jnp.zeros((BLK, HD), bf16)
            colB[p + 4] = jnp.zeros((BLK, HD), f32)

        @pl.when((p < 3) & (seq == 0))
        def _():
            cross_in[0, p] = jnp.zeros((BLK, HD), bf16)
            cross_in[1, p] = jnp.zeros((BLK, HD), bf16)

        @pl.when((p < 3) & (seq == seqs - 1))
        def _():
            QB[p + 8] = jnp.zeros((BLK, HD), bf16)
            GB[p + 8] = jnp.zeros((BLK, HD), bf16)
            rowB[p + 8] = jnp.zeros((8, BLK), f32)

        @pl.when((p >= 4) & (seq == seqs - 1))
        def _():
            cross_in[0, p] = jnp.zeros((BLK, HD), bf16)
            cross_in[1, p] = jnp.zeros((BLK, HD), bf16)

        length = length_ref[block_user(RING * seq + p)]
        inv[p] = 1.0 / jnp.full((8, BLK), length.astype(f32), f32)
        return 0

    lax.fori_loop(0, RING, prepare, 0)
    B_own[...] = jnp.broadcast_to(bucket_ref[...].astype(f32).reshape(1, BLK), (8, BLK))
    load.wait()
    own_live = live_rows(RING * seq + pair)

    def mask_own(n, _):
        rows = pl.ds(pl.multiple_of(n * 32, 32), 32)
        row = lax.broadcasted_iota(i32, (32, RING * HD), 0) + n * 32
        G_own[rows, :] = jnp.where(row < own_live, G_own[rows, :].astype(f32), 0.0).astype(bf16)
        return 0

    lax.fori_loop(0, BLK // 32, mask_own, 0)
    pl.semaphore_wait(barrier, RING - 1 + jnp.where(has_up, 1, 0) + jnp.where(has_down, 1, 0))

    sources = (q_hbm, k_hbm, v_hbm, G_own)

    def head(p):
        return pl.ds(pl.multiple_of(p * HD, HD), HD)

    def bucket_copy(k):
        return pltpu.make_async_remote_copy(
            B_own, B_ring.at[pair], b_send.at[k], b_recv.at[pair], device_id=(seq, place(k)), device_id_type=MESH)

    def in_copy(t, k):
        p = place(k)
        return pltpu.make_async_remote_copy(
            sources[t].at[:, head(p)], rings[t].at[pair], in_send.at[t, k], in_recv.at[t, pair],
            device_id=(seq, p), device_id_type=MESH)

    def self_copy(t):
        return pltpu.make_async_copy(sources[t].at[:, head(pair)], rings[t].at[pair], self_sem.at[t])

    for t in range(4):
        self_copy(t).start()
    self_bucket = pltpu.make_async_copy(B_own, B_ring.at[pair], self_sem.at[4])
    self_bucket.start()

    def send_order(first, second):
        def send(k, tensors):
            for t in tensors:
                in_copy(t, k).start()

        send(1, first + second)

        def near(target, tensors):
            k = 2 + 2 * ((target + core) % 2)
            send(k, tensors)
            send(k + 1, tensors)

        def far(target, tensors):
            send(6 + (target + core) % 2, tensors)

        near(0, first + second)
        far(0, first)
        near(1, first)
        far(0, second)
        far(1, first)
        near(1, second)
        far(1, second)

    def send_buckets(k, _):
        bucket_copy(k).start()
        return 0

    lax.fori_loop(1, RING, send_buckets, 0)

    @pl.when(pair >= 4)
    def _():
        send_order((1, 2), (0, 3))

    @pl.when(pair < 4)
    def _():
        send_order((0, 3), (1, 2))

    for t in range(4):
        self_copy(t).wait()
    self_bucket.wait()

    def wait_in(t, p):
        pltpu.make_async_copy(rings[t].at[p], rings[t].at[p], in_recv.at[t, p]).wait()

    def cross_copies(p, upward):
        if upward:
            pairs = ((KB.at[p], KB.at[p + 4]), (VB.at[p], VB.at[p + 4]), (B_ring.at[p], B_cross.at[p]))
            to = (up, pair)
        else:
            pairs = ((QB.at[p], QB.at[p + 8]), (GB.at[p], GB.at[p + 8]), (B_ring.at[p], B_cross.at[p]))
            to = (down, pair)
        return [
            pltpu.make_async_remote_copy(
                src, dst, x_send.at[n, p], x_recv.at[n, p], device_id=to, device_id_type=MESH)
            for n, (src, dst) in enumerate(pairs)
        ]

    def pass_on(k, _):
        p = source(k)

        @pl.when(k > 0)
        def _():
            pltpu.make_async_copy(B_ring.at[p], B_ring.at[p], b_recv.at[p]).wait()

        @pl.when(p >= 4)
        def _():
            @pl.when(k > 0)
            def _():
                wait_in(1, p)
                wait_in(2, p)

            @pl.when(has_up)
            def _():
                for copy in cross_copies(p, True):
                    copy.start()

        @pl.when(p < 4)
        def _():
            @pl.when(k > 0)
            def _():
                wait_in(0, p)
                wait_in(3, p)

            @pl.when((p < 3) & has_down)
            def _():
                for copy in cross_copies(p, False):
                    copy.start()

        return 0


    half_slope = 0.5 * slope_ref[pair]

    def arrive(k):
        p = source(k)

        @pl.when(k > 0)
        def _():
            @pl.when(p >= 4)
            def _():
                wait_in(0, p)
                wait_in(3, p)

            @pl.when(p < 4)
            def _():
                wait_in(1, p)
                wait_in(2, p)

        row = B_ring[p] * half_slope
        rowB[p] = row
        colB[p] = jnp.broadcast_to(row[0:1], (HD, BLK)).T

        @pl.when((p >= 4) & has_down)
        def _():
            for copy in cross_copies(p, True):
                copy.wait_recv()
            crossed = B_cross[p] * half_slope
            colB[p + 4] = jnp.broadcast_to(crossed[0:1], (HD, BLK)).T

        @pl.when((p < 3) & has_up)
        def _():
            for copy in cross_copies(p, False):
                copy.wait_recv()
            rowB[p + 8] = B_cross[p] * half_slope

    def products(xj, yj, xi, yi):
        return dot(xj, xi, NT), dot(yj, yi, NT)

    def pointwise(raw, d_attn, column, row, weight, mask=None):
        half = raw * (0.5 * SCALE) - jnp.abs(jnp.concatenate([column, column], axis=1) - row)
        th = jnp.tanh(half)
        pw = th * weight + weight
        if mask is not None:
            pw = jnp.where(mask, pw, 0.0)
        aw = half * pw
        return aw.astype(bf16), (d_attn * (pw + aw * (1.0 - th))).astype(bf16)

    def spread(xj, yj, xi, yi, attn, score):
        return dot(attn, yi), dot(score, xi), dot(yj.T, attn), dot(xj.T, score)

    class Diagonal:
        def __init__(self, p):
            self.p = p
            self.operands = (QB[p], GB[p], KB[p], VB[p])

        def first(self):
            self.raw = products(*self.operands)

        def second(self):
            p = self.p
            mask = lax.broadcasted_iota(i32, (BLK, BLK), 0) >= lax.broadcasted_iota(i32, (BLK, BLK), 1)
            self.tiles = pointwise(*self.raw, colB[p], rowB[p][0:1], inv[p][0:1], mask)

        def third(self):
            p = self.p
            uj, wj, ui, wi = spread(*self.operands, *self.tiles)
            OJ[p] += uj
            QJ[p] += wj
            VI[p] += ui
            KI[p] += wi

    class Slot:
        def __init__(self, p, r):
            j, i = jnp.maximum(p, r), jnp.minimum(p, r)
            upper = j >= 4
            ja = jnp.where(upper, j + 4, j)
            ia = jnp.where(upper, i, i + 8)
            base = RING * seq
            user_i, user_j = block_user(base + i), block_user(base + j)
            inside = user_i == user_j
            below = (block_user(base + j - 8) == user_i) & (seq > 0)
            above = (block_user(base + i + 8) == user_j) & (seq < seqs - 1)
            flag = jnp.where(upper, below, above)
            valid = jnp.where(inside | flag, 1.0, 0.0)
            self.on = jnp.where(flag, 1.0, 0.0)
            self.weight = inv[jnp.where(upper, i, j)][0:1] * valid
            self.where = (j, i, ja, ia)

            def pick(a, b):
                return lax.select(flag, a, b)

            self.pick = pick
            self.operands = (pick(KB[ja], QB[j]), pick(VB[ja], GB[j]), pick(QB[ia], KB[i]), pick(GB[ia], VB[i]))

        def first(self):
            self.raw = products(*self.operands)

        def second(self):
            j, i, ja, ia = self.where
            self.tiles = pointwise(
                *self.raw, self.pick(colB[ja], colB[j]), self.pick(rowB[ia], rowB[i])[0:1], self.weight)

        def third(self):
            j, i, ja, ia = self.where
            on, off = self.on, 1.0 - self.on
            uj, wj, ui, wi = spread(*self.operands, *self.tiles)
            OJ[j] += uj * off
            QJ[j] += wj * off
            FJU[j] += uj * on
            FJW[j] += wj * on
            VI[i] += ui * off
            KI[i] += wi * off
            FIU[ia] += ui * on
            FIW[ia] += wi * on

    def together(*tiles):
        count = len(tiles)
        tiles[0].first()
        for n in range(count + 1):
            if n + 1 < count:
                tiles[n + 1].first()
            if n < count:
                tiles[n].second()
            if n >= 1:
                tiles[n - 1].third()

    back = 0.5 * SCALE

    def out_copy(t, p):
        return pltpu.make_async_remote_copy(
            stage.at[t, p], outs[t].at[:, head(pair)], o_send.at[t, p], o_recv.at[t, pair],
            device_id=(seq, p), device_id_type=MESH)

    def out_self(t):
        return pltpu.make_async_copy(stage.at[t, pair], outs[t].at[:, head(pair)], o_self.at[t])

    def emit(t, p):
        @pl.when(p != pair)
        def _():
            out_copy(t, p).start()

        @pl.when(p == pair)
        def _():
            out_self(t).start()

    def return_copies(p, downward):
        to = (down, pair) if downward else (up, pair)
        return [
            pltpu.make_async_remote_copy(
                cross_out.at[n, p], cross_in.at[n, p], r_send.at[n, p], r_recv.at[n, p],
                device_id=to, device_id_type=MESH)
            for n in range(2)
        ]

    def live_mask(p):
        return lax.broadcasted_iota(i32, (BLK, HD), 0) < live_rows(RING * seq + p)

    def finish(p):
        @pl.when(p >= 3)
        def _():
            stage[0, p] = jnp.where(live_mask(p), OJ[p] + FIU[p].T, 0.0).astype(bf16)
            emit(0, p)
            stage[1, p] = ((QJ[p] + FIW[p].T) * back).astype(bf16)
            emit(1, p)

        @pl.when(p < 4)
        def _():
            stage[2, p] = ((KI[p].T + FJW[p]) * back).astype(bf16)
            emit(2, p)
            stage[3, p] = (VI[p].T + FJU[p]).astype(bf16)
            emit(3, p)

        @pl.when(p >= 4)
        def _():
            cross_out[0, p] = FJU[p].astype(bf16)
            cross_out[1, p] = (FJW[p] * back).astype(bf16)

            @pl.when(has_down)
            def _():
                for copy in return_copies(p, True):
                    copy.start()

            FJU[p] = VI[p].T
            FJW[p] = KI[p].T * back

        @pl.when(p < 3)
        def _():
            cross_out[0, p] = FIU[p + 8].T.astype(bf16)
            cross_out[1, p] = (FIW[p + 8].T * back).astype(bf16)

            @pl.when(has_up)
            def _():
                for copy in return_copies(p, False):
                    copy.start()

            OJ[p] = OJ[p] + FIU[p].T
            QJ[p] = (QJ[p] + FIW[p].T) * back

    def step(k, _):
        arrive(k)
        p = source(k)

        def four(m, _):
            together(*[Slot(p, source(4 * m + n)) for n in range(4)])
            return 0

        lax.fori_loop(0, k // 4, four, 0)
        rest = k - k % 4

        @pl.when(k % 4 == 0)
        def _():
            together(Diagonal(p))

        @pl.when(k % 4 == 1)
        def _():
            together(Slot(p, source(rest)), Diagonal(p))

        @pl.when(k % 4 == 2)
        def _():
            together(Slot(p, source(rest)), Slot(p, source(rest + 1)), Diagonal(p))

        @pl.when(k % 4 == 3)
        def _():
            together(*[Slot(p, source(rest + n)) for n in range(3)], Diagonal(p))

        return 0

    def advance(k, _):
        first = jnp.where(k == 0, 0, jnp.where(k == 2, 2, 6))
        end = jnp.where(k == 0, 2, jnp.where(k == 2, 6, jnp.where(k == 4, 8, 6)))
        lax.fori_loop(first, end, pass_on, 0)
        step(k, 0)
        return 0

    lax.fori_loop(0, RING - 1, advance, 0)
    arrive(RING - 1)
    last = source(RING - 1)

    def turn(m):
        return source(jnp.where(m < 5, m + 2, 6 - m))

    def last_two(m, _):
        one, two = turn(2 * m), turn(2 * m + 1)
        together(Slot(last, one), Slot(last, two))
        finish(one)
        finish(two)
        return 0

    lax.fori_loop(0, 3, last_two, 0)
    together(Slot(last, turn(6)), Diagonal(last))
    finish(last)
    finish(turn(6))

    def drain_in(k, _):
        p = source(k)

        @pl.when((p >= 4) & has_up)
        def _():
            for copy in cross_copies(p, True):
                copy.wait_send()

        @pl.when((p < 3) & has_down)
        def _():
            for copy in cross_copies(p, False):
                copy.wait_send()

        @pl.when(k > 0)
        def _():
            bucket_copy(k).wait_send()
            for t in range(4):
                in_copy(t, k).wait_send()

        return 0


    def settle(k, _):
        p = source((k + 2) % RING)

        @pl.when(p >= 4)
        def _():
            @pl.when(has_up)
            def _():
                for copy in return_copies(p, True):
                    copy.wait_recv()

            stage[2, p] = (FJW[p] + cross_in[1, p].astype(f32)).astype(bf16)
            stage[3, p] = (FJU[p] + cross_in[0, p].astype(f32)).astype(bf16)
            emit(2, p)
            emit(3, p)

        @pl.when(p < 3)
        def _():
            @pl.when(has_down)
            def _():
                for copy in return_copies(p, False):
                    copy.wait_recv()

            stage[0, p] = jnp.where(live_mask(p), OJ[p] + cross_in[0, p].astype(f32), 0.0).astype(bf16)
            stage[1, p] = (QJ[p] + cross_in[1, p].astype(f32)).astype(bf16)
            emit(0, p)
            emit(1, p)

        return 0

    lax.fori_loop(0, RING, settle, 0)
    lax.fori_loop(0, RING, drain_in, 0)

    def drain_out(k, _):
        p = source(k)

        @pl.when((p >= 4) & has_down)
        def _():
            for copy in return_copies(p, True):
                copy.wait_send()

        @pl.when((p < 3) & has_up)
        def _():
            for copy in return_copies(p, False):
                copy.wait_send()

        @pl.when(k > 0)
        def _():
            for t in range(4):
                out_copy(t, p).wait_send()
                pltpu.make_async_copy(stage.at[t, p], outs[t].at[:, head(p)], o_recv.at[t, p]).wait()

        return 0

    for t in range(4):
        out_self(t).wait()
    lax.fori_loop(0, RING, drain_out, 0)


def hand_over(*refs):
    ins, outs, held, load, store = refs[:4], refs[4:8], refs[8], refs[9], refs[10]
    half = BLK // 2

    def loads(n):
        rows = pl.ds(n % 2 * half, half)
        return pltpu.make_async_copy(ins[n // 2].at[rows, :], held.at[n], load.at[n])

    def stores(n):
        rows = pl.ds(n % 2 * half, half)
        return pltpu.make_async_copy(held.at[n], outs[n // 2].at[rows, :], store.at[n])

    for n in range(8):
        loads(n).start()
    for n in range(8):
        loads(n).wait()
        stores(n).start()
    for n in range(8):
        stores(n).wait()


def per_device(seqs, queries, keys, values, out_grad, event_bucket, slope, block_user, lengths):
    wide = jax.ShapeDtypeStruct((BLK, RING * HD), bf16)
    hbm = pl.BlockSpec(memory_space=pl.ANY)
    down = lambda n: pltpu.VMEM((n, BLK, HD), f32)
    across = lambda n: pltpu.VMEM((n, HD, BLK), f32)
    dma = pltpu.SemaphoreType.DMA
    results = pl.pallas_call(
        functools.partial(kernel, seqs),
        out_shape=(wide,) * 4,
        in_specs=[hbm] * 8,
        out_specs=(hbm,) * 4,
        scratch_shapes=[
            pltpu.SMEM((RING,), f32),
            pltpu.SMEM((seqs * RING,), i32),
            pltpu.SMEM(lengths.shape, i32),
            pltpu.VMEM((BLK,), i32),
            pltpu.VMEM((11, BLK, HD), bf16),
            pltpu.VMEM((12, BLK, HD), bf16),
            pltpu.VMEM((12, BLK, HD), bf16),
            pltpu.VMEM((11, BLK, HD), bf16),
            pltpu.VMEM((BLK, RING * HD), bf16),
            pltpu.VMEM((8, BLK), f32),
            pltpu.VMEM((8, 8, BLK), f32),
            pltpu.VMEM((8, 8, BLK), f32),
            down(12),
            pltpu.VMEM((11, 8, BLK), f32),
            pltpu.VMEM((8, 8, BLK), f32),
            down(8), down(8), across(8), across(8), down(8), down(8), across(11), across(11),
            pltpu.VMEM((4, 8, BLK, HD), bf16),
            pltpu.VMEM((2, 8, BLK, HD), bf16),
            pltpu.VMEM((2, 8, BLK, HD), bf16),
            dma, dma((4,)), dma((5,)), dma((4, 8)), dma((4, 8)), dma((8,)), dma((8,)), dma((3, 8)), dma((3, 8)),
            dma((2, 8)), dma((2, 8)), dma((4, 8)), dma((4, 8)), dma((4,)),
        ],
        compiler_params=pltpu.CompilerParams(
            collective_id=0, has_side_effects=True, vmem_limit_bytes=62 * 2**20),
        cost_estimate=pl.CostEstimate(
            flops=36 * 6 * 2 * BLK * BLK * HD, bytes_accessed=8 * BLK * RING * HD * 2, transcendentals=36 * BLK * BLK),
    )(slope, block_user, lengths, event_bucket, queries, keys, values, out_grad)
    return pl.pallas_call(
        hand_over,
        out_shape=(wide,) * 4,
        in_specs=[hbm] * 4,
        out_specs=(hbm,) * 4,
        scratch_shapes=[pltpu.VMEM((8, BLK // 2, RING * HD), bf16), dma((8,)), dma((8,))],
        compiler_params=pltpu.CompilerParams(vmem_limit_bytes=62 * 2**20),
    )(*results)


def solution(mesh):
    spread = P(("seq", "pair"), None)
    return jax.shard_map(
        functools.partial(per_device, mesh.shape["seq"]),
        mesh=mesh,
        in_specs=(spread, spread, spread, spread, P(("seq", "pair")), P(), P(), P()),
        out_specs=(spread,) * 4,
        check_vma=False,
    )
```

```python
import functools

import jax
import jax.numpy as jnp
from jax import lax
from jax.experimental import pallas as pl
from jax.experimental.pallas import tpu as pltpu
from jax.sharding import PartitionSpec as P

BLK = 256
HD = 128
RING = 8
MESH = pl.DeviceIdType.MESH
f32, bf16, i32 = jnp.float32, jnp.bfloat16, jnp.int32
SCALE = HD ** -0.5
NN = (((1,), (0,)), ((), ()))
NT = (((1,), (1,)), ((), ()))


def dot(a, b, dims=NN):
    return lax.dot_general(a, b, dims, preferred_element_type=f32)


def kernel(
    seqs, slope_hbm, user_hbm, length_hbm, bucket_hbm, q_hbm, k_hbm, v_hbm, g_hbm,
    o_out, dq_out, dk_out, dv_out,
    slope_ref, user_ref, length_ref, bucket_ref, QB, KB, VB, GB, G_own, B_own, B_ring, B_cross, colB, rowB, inv,
    OJ, QJ, VI, KI, FJU, FJW, FIU, FIW,
    stage, cross_out, cross_in,
    load_sem, small_sem, self_sem, in_send, in_recv, b_send, b_recv, x_send, x_recv, r_send, r_recv, o_send, o_recv, o_self,
):
    seq, pair = lax.axis_index("seq"), lax.axis_index("pair")
    blocks = seqs * RING
    y, core = pair // 2, pair % 2
    up, down = (seq + 1) % seqs, (seq + seqs - 1) % seqs
    has_up, has_down = seq < seqs - 1, seq > 0
    outs = (o_out, dq_out, dk_out, dv_out)
    rings = (QB, KB, VB, GB)

    def offset(k):
        dy = jnp.where(k < 2, 0, jnp.where(k < 6, 1 + 2 * (k % 2), 2))
        dc = jnp.where(k < 2, k, jnp.where(k < 6, k // 4, k - 6))
        return dy, dc

    def place(k):
        dy, dc = offset(k)
        return ((y + dy) % 4) * 2 + (core + dc) % 2

    def source(k):
        dy, dc = offset(k)
        return ((y + 4 - dy) % 4) * 2 + (core + dc) % 2

    barrier = pltpu.get_barrier_semaphore()

    def greet(k, _):
        pl.semaphore_signal(barrier, inc=1, device_id=(seq, place(k)), device_id_type=MESH)
        return 0

    lax.fori_loop(1, RING, greet, 0)

    @pl.when(has_up)
    def _():
        pl.semaphore_signal(barrier, inc=1, device_id=(up, pair), device_id_type=MESH)

    @pl.when(has_down)
    def _():
        pl.semaphore_signal(barrier, inc=1, device_id=(down, pair), device_id_type=MESH)


    load = pltpu.make_async_copy(g_hbm, G_own, load_sem)
    load.start()
    smalls = [
        pltpu.make_async_copy(src, dst, small_sem.at[n])
        for n, (src, dst) in enumerate((
            (user_hbm, user_ref), (length_hbm, length_ref), (slope_hbm, slope_ref), (bucket_hbm, bucket_ref)))
    ]
    for small in smalls:
        small.start()
    for small in smalls:
        small.wait()

    def block_user(block):
        return user_ref[jnp.clip(block, 0, blocks - 1)]

    def live_rows(block):
        user = block_user(block)
        last = (block == blocks - 1) | (block_user(block + 1) != user)
        return jnp.where(last, lax.rem(length_ref[user] - 1, BLK) + 1, BLK)

    def prepare(p, _):
        zero = jnp.zeros((BLK, HD), f32)
        OJ[p] = zero
        QJ[p] = zero
        FJU[p] = zero
        FJW[p] = zero
        zero = jnp.zeros((HD, BLK), f32)
        VI[p] = zero
        KI[p] = zero
        FIU[p] = zero
        FIW[p] = zero

        @pl.when(p < 3)
        def _():
            FIU[8 + p] = zero
            FIW[8 + p] = zero

        @pl.when((p >= 4) & (seq == 0))
        def _():
            KB[p + 4] = jnp.zeros((BLK, HD), bf16)
            VB[p + 4] = jnp.zeros((BLK, HD), bf16)
            colB[p + 4] = jnp.zeros((BLK, HD), f32)

        @pl.when((p < 3) & (seq == 0))
        def _():
            cross_in[0, p] = jnp.zeros((BLK, HD), bf16)
            cross_in[1, p] = jnp.zeros((BLK, HD), bf16)

        @pl.when((p < 3) & (seq == seqs - 1))
        def _():
            QB[p + 8] = jnp.zeros((BLK, HD), bf16)
            GB[p + 8] = jnp.zeros((BLK, HD), bf16)
            rowB[p + 8] = jnp.zeros((8, BLK), f32)

        @pl.when((p >= 4) & (seq == seqs - 1))
        def _():
            cross_in[0, p] = jnp.zeros((BLK, HD), bf16)
            cross_in[1, p] = jnp.zeros((BLK, HD), bf16)

        length = length_ref[block_user(RING * seq + p)]
        inv[p] = 1.0 / jnp.full((8, BLK), length.astype(f32), f32)
        return 0

    lax.fori_loop(0, RING, prepare, 0)
    B_own[...] = jnp.broadcast_to(bucket_ref[...].astype(f32).reshape(1, BLK), (8, BLK))
    load.wait()
    own_live = live_rows(RING * seq + pair)

    def mask_own(n, _):
        rows = pl.ds(pl.multiple_of(n * 32, 32), 32)
        row = lax.broadcasted_iota(i32, (32, RING * HD), 0) + n * 32
        G_own[rows, :] = jnp.where(row < own_live, G_own[rows, :].astype(f32), 0.0).astype(bf16)
        return 0

    lax.fori_loop(0, BLK // 32, mask_own, 0)
    pl.semaphore_wait(barrier, RING - 1 + jnp.where(has_up, 1, 0) + jnp.where(has_down, 1, 0))

    sources = (q_hbm, k_hbm, v_hbm, G_own)

    def head(p):
        return pl.ds(pl.multiple_of(p * HD, HD), HD)

    def bucket_copy(k):
        return pltpu.make_async_remote_copy(
            B_own, B_ring.at[pair], b_send.at[k], b_recv.at[pair], device_id=(seq, place(k)), device_id_type=MESH)

    def in_copy(t, k):
        p = place(k)
        return pltpu.make_async_remote_copy(
            sources[t].at[:, head(p)], rings[t].at[pair], in_send.at[t, k], in_recv.at[t, pair],
            device_id=(seq, p), device_id_type=MESH)

    def self_copy(t):
        return pltpu.make_async_copy(sources[t].at[:, head(pair)], rings[t].at[pair], self_sem.at[t])

    for t in range(4):
        self_copy(t).start()
    self_bucket = pltpu.make_async_copy(B_own, B_ring.at[pair], self_sem.at[4])
    self_bucket.start()

    def send_order(first, second):
        def send(k, tensors):
            for t in tensors:
                in_copy(t, k).start()

        send(1, first + second)

        def near(target, tensors):
            k = 2 + 2 * ((target + core) % 2)
            send(k, tensors)
            send(k + 1, tensors)

        def far(target, tensors):
            send(6 + (target + core) % 2, tensors)

        near(0, first)
        near(0, second)
        far(0, first)
        near(1, first)
        far(0, second)
        far(1, first)
        near(1, second)
        far(1, second)

    def send_buckets(k, _):
        bucket_copy(k).start()
        return 0

    lax.fori_loop(1, RING, send_buckets, 0)

    @pl.when(pair >= 4)
    def _():
        send_order((1, 2), (0, 3))

    @pl.when(pair < 4)
    def _():
        send_order((0, 3), (1, 2))

    for t in range(4):
        self_copy(t).wait()
    self_bucket.wait()

    def wait_in(t, p):
        pltpu.make_async_copy(rings[t].at[p], rings[t].at[p], in_recv.at[t, p]).wait()

    def cross_copies(p, upward):
        if upward:
            pairs = ((KB.at[p], KB.at[p + 4]), (VB.at[p], VB.at[p + 4]), (B_ring.at[p], B_cross.at[p]))
            to = (up, pair)
        else:
            pairs = ((QB.at[p], QB.at[p + 8]), (GB.at[p], GB.at[p + 8]), (B_ring.at[p], B_cross.at[p]))
            to = (down, pair)
        return [
            pltpu.make_async_remote_copy(
                src, dst, x_send.at[n, p], x_recv.at[n, p], device_id=to, device_id_type=MESH)
            for n, (src, dst) in enumerate(pairs)
        ]

    half_slope = 0.5 * slope_ref[pair]

    def pass_on(k, _):
        p = source(k)

        @pl.when(k > 0)
        def _():
            pltpu.make_async_copy(B_ring.at[p], B_ring.at[p], b_recv.at[p]).wait()

        @pl.when(p >= 4)
        def _():
            @pl.when(k > 0)
            def _():
                wait_in(1, p)
                wait_in(2, p)

            @pl.when(has_up)
            def _():
                for copy in cross_copies(p, True):
                    copy.start()

        @pl.when(p < 4)
        def _():
            @pl.when(k > 0)
            def _():
                wait_in(0, p)
                wait_in(3, p)

            @pl.when((p < 3) & has_down)
            def _():
                for copy in cross_copies(p, False):
                    copy.start()

        row = B_ring[p] * half_slope
        rowB[p] = row
        colB[p] = jnp.broadcast_to(row[0:1], (HD, BLK)).T
        return 0


    def arrive(k):
        p = source(k)

        @pl.when(k > 0)
        def _():
            @pl.when(p >= 4)
            def _():
                wait_in(0, p)
                wait_in(3, p)

            @pl.when(p < 4)
            def _():
                wait_in(1, p)
                wait_in(2, p)


        @pl.when((p >= 4) & has_down)
        def _():
            for copy in cross_copies(p, True):
                copy.wait_recv()
            crossed = B_cross[p] * half_slope
            colB[p + 4] = jnp.broadcast_to(crossed[0:1], (HD, BLK)).T

        @pl.when((p < 3) & has_up)
        def _():
            for copy in cross_copies(p, False):
                copy.wait_recv()
            rowB[p + 8] = B_cross[p] * half_slope

    def products(xj, yj, xi, yi):
        return dot(xj, xi, NT), dot(yj, yi, NT)

    def pointwise(raw, d_attn, column, row, weight, mask=None):
        half = raw * (0.5 * SCALE) - jnp.abs(jnp.concatenate([column, column], axis=1) - row)
        th = jnp.tanh(half)
        pw = th * weight + weight
        if mask is not None:
            pw = jnp.where(mask, pw, 0.0)
        aw = half * pw
        return aw.astype(bf16), (d_attn * (pw + aw * (1.0 - th))).astype(bf16)

    def spread(xj, yj, xi, yi, attn, score):
        return dot(attn, yi), dot(score, xi), dot(yj.T, attn), dot(xj.T, score)

    class Diagonal:
        def __init__(self, p):
            self.p = p
            self.operands = (QB[p], GB[p], KB[p], VB[p])

        def first(self):
            self.raw = products(*self.operands)

        def second(self):
            p = self.p
            mask = lax.broadcasted_iota(i32, (BLK, BLK), 0) >= lax.broadcasted_iota(i32, (BLK, BLK), 1)
            self.tiles = pointwise(*self.raw, colB[p], rowB[p][0:1], inv[p][0:1], mask)

        def third(self):
            p = self.p
            uj, wj, ui, wi = spread(*self.operands, *self.tiles)
            OJ[p] += uj
            QJ[p] += wj
            VI[p] += ui
            KI[p] += wi

    class Slot:
        def __init__(self, p, r):
            j, i = jnp.maximum(p, r), jnp.minimum(p, r)
            upper = j >= 4
            ja = jnp.where(upper, j + 4, j)
            ia = jnp.where(upper, i, i + 8)
            base = RING * seq
            user_i, user_j = block_user(base + i), block_user(base + j)
            inside = user_i == user_j
            below = (block_user(base + j - 8) == user_i) & (seq > 0)
            above = (block_user(base + i + 8) == user_j) & (seq < seqs - 1)
            flag = jnp.where(upper, below, above)
            valid = jnp.where(inside | flag, 1.0, 0.0)
            self.on = jnp.where(flag, 1.0, 0.0)
            self.weight = inv[jnp.where(upper, i, j)][0:1] * valid
            self.where = (j, i, ja, ia)

            def pick(a, b):
                return lax.select(flag, a, b)

            self.pick = pick
            self.operands = (pick(KB[ja], QB[j]), pick(VB[ja], GB[j]), pick(QB[ia], KB[i]), pick(GB[ia], VB[i]))

        def first(self):
            self.raw = products(*self.operands)

        def second(self):
            j, i, ja, ia = self.where
            self.tiles = pointwise(
                *self.raw, self.pick(colB[ja], colB[j]), self.pick(rowB[ia], rowB[i])[0:1], self.weight)

        def third(self):
            j, i, ja, ia = self.where
            on, off = self.on, 1.0 - self.on
            uj, wj, ui, wi = spread(*self.operands, *self.tiles)
            OJ[j] += uj * off
            QJ[j] += wj * off
            FJU[j] += uj * on
            FJW[j] += wj * on
            VI[i] += ui * off
            KI[i] += wi * off
            FIU[ia] += ui * on
            FIW[ia] += wi * on

    def together(*tiles):
        count = len(tiles)
        tiles[0].first()
        for n in range(count + 1):
            if n + 1 < count:
                tiles[n + 1].first()
            if n < count:
                tiles[n].second()
            if n >= 1:
                tiles[n - 1].third()

    back = 0.5 * SCALE

    def out_copy(t, p):
        return pltpu.make_async_remote_copy(
            stage.at[t, p], outs[t].at[:, head(pair)], o_send.at[t, p], o_recv.at[t, pair],
            device_id=(seq, p), device_id_type=MESH)

    def out_self(t):
        return pltpu.make_async_copy(stage.at[t, pair], outs[t].at[:, head(pair)], o_self.at[t])

    def emit(t, p):
        @pl.when(p != pair)
        def _():
            out_copy(t, p).start()

        @pl.when(p == pair)
        def _():
            out_self(t).start()

    def return_copies(p, downward):
        to = (down, pair) if downward else (up, pair)
        return [
            pltpu.make_async_remote_copy(
                cross_out.at[n, p], cross_in.at[n, p], r_send.at[n, p], r_recv.at[n, p],
                device_id=to, device_id_type=MESH)
            for n in range(2)
        ]

    def live_mask(p):
        return lax.broadcasted_iota(i32, (BLK, HD), 0) < live_rows(RING * seq + p)

    def finish(p):
        @pl.when(p >= 3)
        def _():
            stage[0, p] = jnp.where(live_mask(p), OJ[p] + FIU[p].T, 0.0).astype(bf16)
            emit(0, p)
            stage[1, p] = ((QJ[p] + FIW[p].T) * back).astype(bf16)
            emit(1, p)

        @pl.when(p < 4)
        def _():
            stage[2, p] = ((KI[p].T + FJW[p]) * back).astype(bf16)
            emit(2, p)
            stage[3, p] = (VI[p].T + FJU[p]).astype(bf16)
            emit(3, p)

        @pl.when(p >= 4)
        def _():
            cross_out[0, p] = FJU[p].astype(bf16)
            cross_out[1, p] = (FJW[p] * back).astype(bf16)

            @pl.when(has_down)
            def _():
                for copy in return_copies(p, True):
                    copy.start()

            FJU[p] = VI[p].T
            FJW[p] = KI[p].T * back

        @pl.when(p < 3)
        def _():
            cross_out[0, p] = FIU[p + 8].T.astype(bf16)
            cross_out[1, p] = (FIW[p + 8].T * back).astype(bf16)

            @pl.when(has_up)
            def _():
                for copy in return_copies(p, False):
                    copy.start()

            OJ[p] = OJ[p] + FIU[p].T
            QJ[p] = (QJ[p] + FIW[p].T) * back

    def step(k, _):
        arrive(k)
        p = source(k)

        def four(m, _):
            together(*[Slot(p, source(4 * m + n)) for n in range(4)])
            return 0

        lax.fori_loop(0, k // 4, four, 0)
        rest = k - k % 4

        @pl.when(k % 4 == 0)
        def _():
            together(Diagonal(p))

        @pl.when(k % 4 == 1)
        def _():
            together(Slot(p, source(rest)), Diagonal(p))

        @pl.when(k % 4 == 2)
        def _():
            together(Slot(p, source(rest)), Slot(p, source(rest + 1)), Diagonal(p))

        @pl.when(k % 4 == 3)
        def _():
            together(*[Slot(p, source(rest + n)) for n in range(3)], Diagonal(p))

        return 0

    def advance(k, _):
        first = jnp.where(k == 0, 0, jnp.where(k == 2, 2, 6))
        end = jnp.where(k == 0, 2, jnp.where(k == 2, 6, jnp.where(k == 4, 8, 6)))
        lax.fori_loop(first, end, pass_on, 0)
        step(k, 0)
        return 0

    lax.fori_loop(0, RING - 1, advance, 0)
    arrive(RING - 1)
    last = source(RING - 1)

    def turn(m):
        return source(jnp.where(m < 5, m + 2, 6 - m))

    def last_two(m, _):
        one, two = turn(2 * m), turn(2 * m + 1)
        together(Slot(last, one), Slot(last, two))
        finish(one)
        finish(two)
        return 0

    lax.fori_loop(0, 3, last_two, 0)
    together(Slot(last, turn(6)), Diagonal(last))
    finish(last)
    finish(turn(6))

    def drain_in(k, _):
        p = source(k)

        @pl.when((p >= 4) & has_up)
        def _():
            for copy in cross_copies(p, True):
                copy.wait_send()

        @pl.when((p < 3) & has_down)
        def _():
            for copy in cross_copies(p, False):
                copy.wait_send()

        @pl.when(k > 0)
        def _():
            bucket_copy(k).wait_send()
            for t in range(4):
                in_copy(t, k).wait_send()

        return 0


    def settle(k, _):
        p = source((k + 2) % RING)

        @pl.when(p >= 4)
        def _():
            @pl.when(has_up)
            def _():
                for copy in return_copies(p, True):
                    copy.wait_recv()

            stage[2, p] = (FJW[p] + cross_in[1, p].astype(f32)).astype(bf16)
            stage[3, p] = (FJU[p] + cross_in[0, p].astype(f32)).astype(bf16)
            emit(2, p)
            emit(3, p)

        @pl.when(p < 3)
        def _():
            @pl.when(has_down)
            def _():
                for copy in return_copies(p, False):
                    copy.wait_recv()

            stage[0, p] = jnp.where(live_mask(p), OJ[p] + cross_in[0, p].astype(f32), 0.0).astype(bf16)
            stage[1, p] = (QJ[p] + cross_in[1, p].astype(f32)).astype(bf16)
            emit(0, p)
            emit(1, p)

        return 0

    lax.fori_loop(0, RING, settle, 0)
    lax.fori_loop(0, RING, drain_in, 0)

    def drain_out(k, _):
        p = source(k)

        @pl.when((p >= 4) & has_down)
        def _():
            for copy in return_copies(p, True):
                copy.wait_send()

        @pl.when((p < 3) & has_up)
        def _():
            for copy in return_copies(p, False):
                copy.wait_send()

        @pl.when(k > 0)
        def _():
            for t in range(4):
                out_copy(t, p).wait_send()
                pltpu.make_async_copy(stage.at[t, p], outs[t].at[:, head(p)], o_recv.at[t, p]).wait()

        return 0

    for t in range(4):
        out_self(t).wait()
    lax.fori_loop(0, RING, drain_out, 0)


def hand_over(*refs):
    ins, outs, held, load, store = refs[:4], refs[4:8], refs[8], refs[9], refs[10]
    half = BLK // 2

    def loads(n):
        rows = pl.ds(n % 2 * half, half)
        return pltpu.make_async_copy(ins[n // 2].at[rows, :], held.at[n], load.at[n])

    def stores(n):
        rows = pl.ds(n % 2 * half, half)
        return pltpu.make_async_copy(held.at[n], outs[n // 2].at[rows, :], store.at[n])

    for n in range(8):
        loads(n).start()
    for n in range(8):
        loads(n).wait()
        stores(n).start()
    for n in range(8):
        stores(n).wait()


def per_device(seqs, queries, keys, values, out_grad, event_bucket, slope, block_user, lengths):
    wide = jax.ShapeDtypeStruct((BLK, RING * HD), bf16)
    hbm = pl.BlockSpec(memory_space=pl.ANY)
    down = lambda n: pltpu.VMEM((n, BLK, HD), f32)
    across = lambda n: pltpu.VMEM((n, HD, BLK), f32)
    dma = pltpu.SemaphoreType.DMA
    results = pl.pallas_call(
        functools.partial(kernel, seqs),
        out_shape=(wide,) * 4,
        in_specs=[hbm] * 8,
        out_specs=(hbm,) * 4,
        scratch_shapes=[
            pltpu.SMEM((RING,), f32),
            pltpu.SMEM((seqs * RING,), i32),
            pltpu.SMEM(lengths.shape, i32),
            pltpu.VMEM((BLK,), i32),
            pltpu.VMEM((11, BLK, HD), bf16),
            pltpu.VMEM((12, BLK, HD), bf16),
            pltpu.VMEM((12, BLK, HD), bf16),
            pltpu.VMEM((11, BLK, HD), bf16),
            pltpu.VMEM((BLK, RING * HD), bf16),
            pltpu.VMEM((8, BLK), f32),
            pltpu.VMEM((8, 8, BLK), f32),
            pltpu.VMEM((8, 8, BLK), f32),
            down(12),
            pltpu.VMEM((11, 8, BLK), f32),
            pltpu.VMEM((8, 8, BLK), f32),
            down(8), down(8), across(8), across(8), down(8), down(8), across(11), across(11),
            pltpu.VMEM((4, 8, BLK, HD), bf16),
            pltpu.VMEM((2, 8, BLK, HD), bf16),
            pltpu.VMEM((2, 8, BLK, HD), bf16),
            dma, dma((4,)), dma((5,)), dma((4, 8)), dma((4, 8)), dma((8,)), dma((8,)), dma((3, 8)), dma((3, 8)),
            dma((2, 8)), dma((2, 8)), dma((4, 8)), dma((4, 8)), dma((4,)),
        ],
        compiler_params=pltpu.CompilerParams(
            collective_id=0, has_side_effects=True, vmem_limit_bytes=62 * 2**20),
        cost_estimate=pl.CostEstimate(
            flops=36 * 6 * 2 * BLK * BLK * HD, bytes_accessed=8 * BLK * RING * HD * 2, transcendentals=36 * BLK * BLK),
    )(slope, block_user, lengths, event_bucket, queries, keys, values, out_grad)
    return pl.pallas_call(
        hand_over,
        out_shape=(wide,) * 4,
        in_specs=[hbm] * 4,
        out_specs=(hbm,) * 4,
        scratch_shapes=[pltpu.VMEM((8, BLK // 2, RING * HD), bf16), dma((8,)), dma((8,))],
        compiler_params=pltpu.CompilerParams(vmem_limit_bytes=62 * 2**20),
    )(*results)


def solution(mesh):
    spread = P(("seq", "pair"), None)
    return jax.shard_map(
        functools.partial(per_device, mesh.shape["seq"]),
        mesh=mesh,
        in_specs=(spread, spread, spread, spread, P(("seq", "pair")), P(), P(), P()),
        out_specs=(spread,) * 4,
        check_vma=False,
    )
```
